32 devices in a mesh: row: 8 (over z, x), col: 4 (over y, core).
Axes of the slice: x: 2, y: 2, z: 4, core: 2. Of those that a mesh axis runs over, the one named last changes fastest.
Arguments:
- coeffs: float32 [4096, 128], P(('row', 'col')), may hold values from -6 to 6
- basis: float32 [64, 32, 4096], P('row', 'col'), may hold values from -0.125 to 0.125
- observed: float32 [64, 32, 128], P('row', 'col'), may hold values from -6 to 6
- lift_w: float32 [32], replicated, may hold values from -3 to 3
- lift_b: float32 [32], replicated, may hold values from -3 to 3
- w_one: bfloat16 [3, 3, 32, 32], replicated, may hold values from -0.375 to 0.375
- b_one: float32 [32], replicated, may hold values from -3 to 3
- w_two: bfloat16 [3, 3, 32, 32], replicated, may hold values from -0.375 to 0.375
- b_two: float32 [32], replicated, may hold values from -3 to 3
- read_w: float32 [32], replicated, may hold values from -1 to 1
Outputs:
- pressure: float32 [64, 32, 128], P('row', 'col')
- grad_coeffs: float32 [4096, 128], P(('row', 'col'))
The draws below stay inside these ranges and needn't reach their ends.
All inputs are finite; a program needn't handle non-finite values.
Results may differ from the reference program's by a relative error of at most 0.015.
Values may be sent and summed in bfloat16 or wider, within the bound.
A program may use at most 64 MiB of HBM per device.

```python
import math
import jax
import jax.numpy as jnp
from jax import lax

M = 4096
C = 32
B = 128
NX = 64
NY = 32


def with_spikes(drawn, rng, source, target, blocks, factor):
    owner, partner = [(jnp.arange(drawn.shape[axis_at]) // (drawn.shape[axis_at] // blocks)).reshape([-1 if axis == axis_at else 1 for axis in range(drawn.ndim)]) for axis_at in (source, target)]
    chosen = jax.random.permutation(rng, blocks)[partner]
    strong = (owner == chosen) | (owner == (partner + blocks // 2) % blocks)
    return jnp.where(strong, factor * drawn, drawn)


def shard_levels(stream_key, extent, split, smallest, high):
    gain, own = 1.0, jax.random.fold_in(stream_key, 6)
    for dim, parts in split:
        heights = jnp.exp(jax.random.uniform(jax.random.fold_in(own, dim), (parts,), jnp.float32, smallest / len(split), high / len(split)))
        gain = gain * jnp.repeat(heights, extent[dim] // parts).reshape([-1 if axis == dim else 1 for axis in range(len(extent))])
    return gain


def noise(own_key, shape, deviation, most, shards=(), kind=jnp.bfloat16):
    entries = jax.random.normal(own_key, shape, jnp.float32) * deviation
    if len(shards) > 0:
        entries = shard_levels(own_key, shape, shards, -0.22, 0.18) * entries
    return jnp.clip(entries, min=-most, max=most).astype(kind)


def gaussian_with(key, dims, width, reach, shards, heavy, kind=jnp.bfloat16):
    entries = width * jax.random.normal(key, dims, jnp.float32)
    if shards:
        entries = entries * shard_levels(key, dims, shards, -0.22, 0.18)
    return jnp.clip(with_spikes(entries, jax.random.fold_in(key, 3), *heavy), -reach, reach).astype(kind)


def setup_inputs(seed: int = 0) -> dict:
    arg_keys = jax.random.split(jax.random.key(seed), 11)
    coeffs = noise(arg_keys[0], (M, B), 1.0, 6.0, ((0, 32),), jnp.float32)
    basis = gaussian_with(arg_keys[1], (NX, NY, M), M ** -0.5, 0.125, ((0, 8), (1, 4)), (0, 2, 8, 2.0), jnp.float32)
    observed = noise(arg_keys[2], (NX, NY, B), 1.0, 6.0, ((0, 8), (1, 4)), jnp.float32)
    lift_w = noise(arg_keys[3], (C,), 1.0, 3.0, (), jnp.float32)
    lift_b = noise(arg_keys[4], (C,), 0.5, 3.0, (), jnp.float32)
    w_one = noise(arg_keys[5], (3, 3, C, C), (9 * C) ** -0.5, 0.375)
    b_one = noise(arg_keys[6], (C,), 0.3, 3.0, (), jnp.float32)
    w_two = noise(arg_keys[7], (3, 3, C, C), (9 * C) ** -0.5, 0.375)
    b_two = noise(arg_keys[8], (C,), 0.3, 3.0, (), jnp.float32)
    read_w = noise(arg_keys[9], (C,), C ** -0.5, 1.0, (), jnp.float32)
    return {"coeffs": coeffs, "basis": basis, "observed": observed, "lift_w": lift_w, "lift_b": lift_b, "w_one": w_one, "b_one": b_one, "w_two": w_two, "b_two": b_two, "read_w": read_w}


prior_weight = 0.1


def conv_fwd(values, weights):
    padded = jnp.pad(values.astype(jnp.float32), ((1, 1), (1, 1), (0, 0), (0, 0)))
    nrow = values.shape[0]
    ncol = values.shape[1]
    running = jnp.zeros(values.shape[:3] + (weights.shape[3],), jnp.float32)
    for shift_x in range(3):
        for shift_y in range(3):
            window = padded[shift_x:shift_x + nrow, shift_y:shift_y + ncol]
            running = running + jnp.einsum("xybi,io->xybo", window, weights[shift_x, shift_y].astype(jnp.float32))
    return running


def conv_back(grads, weights):
    padded = jnp.pad(grads.astype(jnp.float32), ((1, 1), (1, 1), (0, 0), (0, 0)))
    nrow = grads.shape[0]
    ncol = grads.shape[1]
    running = jnp.zeros(grads.shape[:3] + (weights.shape[2],), jnp.float32)
    for shift_x in range(3):
        for shift_y in range(3):
            window = padded[2 - shift_x:2 - shift_x + nrow, 2 - shift_y:2 - shift_y + ncol]
            running = running + jnp.einsum("xybo,io->xybi", window, weights[shift_x, shift_y].astype(jnp.float32))
    return running


def reference(coeffs, basis, observed, lift_w, lift_b, w_one, b_one, w_two, b_two, read_w):
    flat_basis = basis.reshape(NX * NY, M)
    logperm = jnp.dot(flat_basis, coeffs, precision=lax.Precision.HIGHEST, preferred_element_type=jnp.float32)
    block_size = math.gcd(B, 8)
    nblocks = B // block_size
    field_blocks = jnp.moveaxis(logperm.reshape(NX, NY, nblocks, block_size), 2, 0)
    obs_blocks = jnp.moveaxis(observed.reshape(NX, NY, nblocks, block_size), 2, 0)

    def surrogate(pair):
        field_vals, obs_vals = pair
        lifted = (field_vals[..., None] * lift_w + lift_b).astype(jnp.bfloat16)
        hidden_one = jnp.tanh(conv_fwd(lifted, w_one) + b_one).astype(jnp.bfloat16)
        hidden_two = jnp.tanh(conv_fwd(hidden_one, w_two) + b_two)
        press = jnp.sum(hidden_two * read_w, axis=-1)
        misfit = press - obs_vals
        grad_two = (misfit[..., None] * read_w * (1.0 - hidden_two * hidden_two)).astype(jnp.bfloat16)
        h_one = hidden_one.astype(jnp.float32)
        grad_one = (conv_back(grad_two, w_two) * (1.0 - h_one * h_one)).astype(jnp.bfloat16)
        grad_field = jnp.sum(conv_back(grad_one, w_one) * lift_w, axis=-1)
        return press, grad_field

    press_blocks, grad_blocks = lax.map(surrogate, (field_blocks, obs_blocks))
    pressure = jnp.moveaxis(press_blocks, 0, 2).reshape(NX, NY, B)
    grad_field = jnp.moveaxis(grad_blocks, 0, 2).reshape(NX * NY, B)
    grad_coeffs = jnp.dot(flat_basis.T, grad_field, precision=lax.Precision.HIGHEST, preferred_element_type=jnp.float32) + prior_weight * coeffs
    return pressure, grad_coeffs
```

```python
import functools

import jax
import jax.numpy as jnp
import numpy as np
from jax import lax
from jax.experimental import pallas as pl
from jax.experimental.pallas import tpu as pltpu
from jax.sharding import PartitionSpec as P

prior_weight = 0.1
MESH = pl.DeviceIdType.MESH
bf16 = jnp.bfloat16
f32 = jnp.float32


def stacked_taps(base, count):
    rows = [
        jnp.pad(base, ((0, 0), (0, 0), (32 * k, 32 * (count - 1 - k)))) for k in range(count)
    ]
    return jnp.concatenate(rows, axis=1)


def weights(lift_w, lift_b, w_one, b_one, w_two):
    one = w_one.astype(f32)
    lift = jnp.sum(one * lift_w[:, None], axis=2)
    shift = jnp.sum(one * lift_b[:, None], axis=2)
    place = np.zeros((14, 3, 24), np.float32)
    for y in range(14):
        for q in range(3):
            place[y, q, y + q + 4] = 1.0
    spread = lambda v: sum(
        place[None, :, q, None, :] * v[:, q][:, None, :, None] for q in range(3)
    ).reshape(3, 448, 24)
    on_field = spread(lift)
    on_mask = spread(shift)
    hi = b_one.astype(bf16).astype(f32)
    bias = jnp.stack([hi, b_one - hi], axis=1)
    bias = jnp.pad(jnp.tile(bias, (14, 1))[None], ((0, 2), (0, 0), (0, 6)))
    first = jnp.concatenate([on_field, on_field, on_mask, bias], axis=2)
    first = jnp.transpose(first, (1, 0, 2)).reshape(448, 240).astype(bf16)
    ahead = stacked_taps(jnp.transpose(w_two, (0, 3, 1, 2)).reshape(3, 32, 96), 4)
    turned = w_two[::-1, ::-1]
    back = stacked_taps(jnp.transpose(turned, (0, 2, 1, 3)).reshape(3, 32, 96), 4)
    place = np.zeros((8, 3, 10), np.float32)
    for y in range(8):
        for q in range(3):
            place[y, q, y + q] = 1.0
    flip = lift[::-1, ::-1]
    last = sum(
        place[None, :, q, :, None] * flip[:, q][:, None, None, :] for q in range(3)
    ).reshape(24, 320)
    return first, ahead, back, last.astype(bf16)


def kernel(
    sizes, coeffs, basis, observed, first, ahead, back, last, bias_two, read,
    pressure, grad,
    gath, turned, field, obs, stack, hid, gtwo, gone, press_ext, own, own_half,
    away, away_in, a_send, a_in, b_send, b_in, a_sum, b_sum, c_send, c_in, d_send, d_in,
    z_send, z_in,
    g_ss, g_rs, h_ss, h_rs, r_ss, r_rs,
):
    R, N, Z, X, Y, half = sizes
    row, col = lax.axis_index("row"), lax.axis_index("col")
    z, x = row // X, row % X
    y, c = col // 2, col % 2
    mp = 2 * half
    cells, modes = basis.shape

    z_to = [((lax.rem(z + k, Z) * X + x, col), lax.rem(z + k, Z)) for k in range(1, Z)]
    x_to = [((z * X + lax.rem(x + k, X), col), lax.rem(x + k, X)) for k in range(1, X)]
    y_to = [((row, lax.rem(y + k, Y) * 2 + c), lax.rem(y + k, Y)) for k in range(1, Y)]
    c_to = (row, y * 2 + 1 - c)
    sides = [(dx, dy) for dx in (-1, 0, 1) for dy in (-1, 0, 1) if (dx, dy) != (0, 0)]

    def exists(dx, dy):
        return (row + dx >= 0) & (row + dx < R) & (col + dy >= 0) & (col + dy < N)

    field[...] = jnp.zeros(field.shape, f32)
    obs[...] = jnp.zeros(obs.shape, f32)

    barrier = pltpu.get_barrier_semaphore()
    expect = (Z - 1) + (X - 1) + (Y - 1) + 1
    for dev in [d for d, _ in z_to + x_to + y_to] + [c_to]:
        pl.semaphore_signal(barrier, inc=1, device_id=dev, device_id_type=MESH)
    for dx, dy in sides:
        there = exists(dx, dy)

        @pl.when(there)
        def _():
            pl.semaphore_signal(
                barrier, inc=1, device_id=(row + dx, col + dy), device_id_type=MESH
            )

        expect = expect + there.astype(jnp.int32)
    gath[z, x, y, c] = coeffs[...].reshape(2, half, 128).astype(bf16)
    pl.semaphore_wait(barrier, expect)

    def push(src, dst, ss, rs, dev):
        copy = pltpu.make_async_remote_copy(
            src_ref=src, dst_ref=dst, send_sem=ss, recv_sem=rs, device_id=dev,
            device_id_type=MESH,
        )
        copy.start()
        return copy

    sent = []
    n_gath = [0]

    def spread(ref, peers):
        made = []
        for dev, _ in peers:
            k = n_gath[0]
            n_gath[0] += 1
            made.append(push(ref, ref, g_ss.at[k], g_rs.at[k], dev))
        sent.extend(made)
        return made

    def rim(buf, tile, width, base):
        def parts(dx, dy):
            src = tile if dx == 0 else (
                tile.at[pl.ds(0, width)] if dx < 0 else tile.at[pl.ds(8 - width, width)]
            )
            at = pl.ds(width, 8) if dx == 0 else (
                pl.ds(8 + width, width) if dx < 0 else pl.ds(0, width)
            )
            return src, buf.at[1 - dy, at]

        def do(k, dx, dy):
            src, dst = parts(dx, dy)
            return pltpu.make_async_remote_copy(
                src_ref=src, dst_ref=dst, send_sem=h_ss.at[base + k],
                recv_sem=h_rs.at[base + k], device_id=(row + dx, col + dy),
                device_id_type=MESH,
            )

        def start():
            for k, (dx, dy) in enumerate(sides):
                @pl.when(exists(dx, dy))
                def _():
                    do(k, dx, dy).start()

        def wait_in():
            for k, (dx, dy) in enumerate(sides):
                @pl.when(exists(-dx, -dy))
                def _():
                    do(k, dx, dy).wait_recv()

        def wait_out():
            for k, (dx, dy) in enumerate(sides):
                @pl.when(exists(dx, dy))
                def _():
                    do(k, dx, dy).wait_send()

        return start, wait_in, wait_out

    stage = spread(gath.at[z, x, y, c], z_to)
    obs_start, obs_in, obs_out = rim(obs, observed, 2, 0)
    obs_start()
    obs[1, 2:10] = observed[...]

    @pl.loop(0, modes // 512)
    def _(i):
        at = pl.multiple_of(i * 512, 512)
        turned[pl.ds(at, 512), :] = basis[:, pl.ds(at, 512)].T.astype(bf16)

    for copy in stage:
        copy.wait_recv()
    stage_a = spread(gath.at[:, x, y, c, 0], x_to)
    stage_b = spread(gath.at[:, x, y, c, 1], y_to)
    for copy in stage_a:
        copy.wait_recv()
    stage_a = spread(gath.at[:, :, y, c, 0], y_to)
    for copy in stage_b:
        copy.wait_recv()
    stage_b = spread(gath.at[:, x, :, c, 1], x_to)
    for copy in stage_a + stage_b:
        copy.wait_recv()
    stage = spread(gath.at[:, :, :, c], [(c_to, None)])
    for copy in stage:
        copy.wait_recv()

    tiles = 512 // mp
    group = X * Y * 2

    own_field = jnp.zeros((cells, 128), f32)
    for iz in range(Z):
        block = gath[iz].reshape(group * mp, 128)
        own_field = own_field + jnp.dot(
            basis[:, iz * group * mp : (iz + 1) * group * mp].astype(bf16), block,
            preferred_element_type=f32,
        )
    tile = press_ext.at[pl.ds(0, 8)]
    press_ext[0:8] = own_field.reshape(8, 8, 128)
    field[1, 4:12] = own_field.reshape(8, 8, 128)
    field_start, field_in, field_out = rim(field, tile, 4, 8)
    field_start()
    field_in()
    obs_in()
    field_out()
    obs_out()

    ones = jnp.ones((8, 128), f32)
    y_at = lax.broadcasted_iota(jnp.int32, (24, 128), 0) + (col * 8 - 8)
    y_in = (y_at >= 0) & (y_at < N * 8)

    @pl.loop(0, 16)
    def _(i):
        values = jnp.concatenate([field[0, i], field[1, i], field[2, i]], axis=0)
        hi = values.astype(bf16).astype(f32)
        xg = row * 8 + i - 4
        inside = jnp.where(y_in & (xg >= 0) & (xg < R * 8), 1.0, 0.0)
        full = jnp.concatenate([hi, values - hi, inside, ones], axis=0)
        stack[pl.ds(pl.multiple_of(i * 80, 16), 80), :] = full.astype(bf16)

    def inside(count, off, xg):
        at = lax.broadcasted_iota(jnp.int32, (count * 32, 128), 0)
        low = (off - col * 8) * 32
        high = jnp.where((xg >= 0) & (xg < R * 8), low + N * 256, -1)
        return (at >= low) & (at < high)

    @pl.loop(0, 14)
    def _(i):
        rows = stack[pl.ds(pl.multiple_of(i * 80, 16), 240), :]
        acc = jnp.dot(first[...], rows, preferred_element_type=f32)
        value = jnp.where(inside(14, 3, row * 8 + i - 3), jnp.tanh(acc), 0.0)
        hid[:, pl.ds(pl.multiple_of(i * 128, 128), 128)] = value.astype(bf16)

    def conv(w, src, starts, at):
        out = []
        for s in starts:
            acc = None
            for k in range(3):
                v = src[s * 32 : s * 32 + 192, pl.ds(pl.multiple_of(at + k * 128, 128), 256)]
                d = jnp.dot(w[k], v, preferred_element_type=f32)
                acc = d if acc is None else acc + d
            out.append(acc)
        return out

    @pl.loop(0, 6)
    def _(i):
        at = i * 256
        acc = jnp.concatenate(conv(ahead, hid, (0, 4, 8), at), axis=0)
        for s in range(2):
            xi = i * 2 + s
            t = jnp.tanh(acc[:, s * 128 : s * 128 + 128] + bias_two[...])
            pr = jnp.sum((t * read[...]).reshape(12, 32, 128), axis=1)
            seen = jnp.concatenate([obs[0, xi], obs[1, xi], obs[2, xi]], axis=0)[6:18]
            miss = jnp.broadcast_to((pr - seen)[:, None, :], (12, 32, 128)).reshape(384, 128)
            g = miss * read[...] * (1.0 - t * t)
            g = jnp.where(inside(12, 2, row * 8 + xi - 2), g, 0.0)
            gtwo[:, pl.ds(pl.multiple_of(at + s * 128, 128), 128)] = g.astype(bf16)
            press_ext[xi] = pr[2:10]

    pressure[...] = press_ext[2:10]

    @pl.loop(0, 5)
    def _(i):
        at = i * 256
        a0, a1, a2 = conv(back, gtwo, (0, 4, 6), at)
        acc = jnp.concatenate([a0, a1, a2[64:]], axis=0)
        for s in range(2):
            xi = i * 2 + s
            h = hid[64:384, pl.ds(pl.multiple_of(at + (2 + s) * 128, 128), 128)].astype(f32)
            g = acc[:, s * 128 : s * 128 + 128] * (1.0 - h * h)
            g = jnp.where(inside(10, 1, row * 8 + xi - 1), g, 0.0)
            gone[:, pl.ds(pl.multiple_of(at + s * 128, 128), 128)] = g.astype(bf16)

    parts = jnp.dot(last[...], gone[...], preferred_element_type=f32)
    slabs = [
        sum(parts[8 * k : 8 * k + 8, (xi + k) * 128 : (xi + k + 1) * 128] for k in range(3))
        for xi in range(8)
    ]
    grad_field = jnp.concatenate(slabs, axis=0).astype(bf16)

    def project(core, into, kind):
        @pl.loop(0, Z * X * Y)
        def _(j):
            at = pl.multiple_of((j * 2 + core) * mp, mp)
            d = jnp.dot(turned[pl.ds(at, mp), :], grad_field, preferred_element_type=f32)
            jz, jr = j // (X * Y), j % (X * Y)
            into[jz, jr // Y, jr % Y] = d.reshape(2, half, 128).astype(kind)

    n_red = [0]

    def shed(src_at, slots, peers):
        made = []
        for k, (dev, peer) in enumerate(peers):
            i = n_red[0]
            n_red[0] += 1
            made.append(push(src_at(peer), slots.at[k], r_ss.at[i], r_rs.at[i], dev))
        sent.extend(made)
        return made

    project(1 - c, away, bf16)
    stage = shed(lambda _: away, away_in, [(c_to, None)])
    project(c, own, f32)
    for copy in stage:
        copy.wait_recv()
    own[...] = own[...] + away_in[0].astype(f32)
    own_half[...] = own[...].astype(bf16)
    stage_a = shed(lambda p: own_half.at[:, :, p, 0], a_in, y_to)
    stage_b = shed(lambda p: own_half.at[:, p, :, 1], b_in, x_to)
    for copy in stage_a:
        copy.wait_recv()
    total = own[:, :, y, 0]
    for k in range(Y - 1):
        total = total + a_in[k].astype(f32)
    a_sum[...] = total
    c_send[...] = total.astype(bf16)
    stage_a = shed(lambda p: c_send.at[:, p], c_in, x_to)
    for copy in stage_b:
        copy.wait_recv()
    total = own[:, x, :, 1]
    for k in range(X - 1):
        total = total + b_in[k].astype(f32)
    b_sum[...] = total
    d_send[...] = total.astype(bf16)
    stage_b = shed(lambda p: d_send.at[:, p], d_in, y_to)
    for copy in stage_a + stage_b:
        copy.wait_recv()
    part_a, part_b = a_sum[:, x], b_sum[:, y]
    for k in range(X - 1):
        part_a = part_a + c_in[k].astype(f32)
    for k in range(Y - 1):
        part_b = part_b + d_in[k].astype(f32)
    own[:, 0, 0, 0] = part_a
    own[:, 0, 0, 1] = part_b
    z_send[:, 0] = part_a.astype(bf16)
    z_send[:, 1] = part_b.astype(bf16)
    stage = shed(lambda p: z_send.at[p], z_in, z_to)
    for copy in stage:
        copy.wait_recv()
    total = own[z, 0, 0]
    for k in range(Z - 1):
        total = total + z_in[k].astype(f32)
    grad[...] = total.reshape(mp, 128) + prior_weight * coeffs[...]
    for copy in sent:
        copy.wait_send()


def shards(sizes, coeffs, basis, observed, lift_w, lift_b, w_one, b_one, w_two, b_two, read_w):
    R, N, Z, X, Y = sizes
    mode_count, batch = basis.shape[2], coeffs.shape[1]
    own = coeffs.shape[0]
    mp = max(own, 32)
    half = mp // 2
    flat = basis.reshape(64, mode_count)
    if mp != own:
        flat = jnp.pad(flat.reshape(64, R * N, own), ((0, 0), (0, 0), (0, mp - own)))
        flat = flat.reshape(64, R * N * mp)
        coeffs = jnp.pad(coeffs, ((0, mp - own), (0, 0)))
    modes = R * N * mp
    first, ahead, back, last = weights(lift_w, lift_b, w_one, b_one, w_two)
    vmem = pl.BlockSpec(memory_space=pltpu.VMEM)
    block = (half, batch)
    gathers = (Z - 1) + 2 * (X - 1) + 2 * (Y - 1) + 1
    V = pltpu.VMEM
    pressure, grad = pl.pallas_call(
        functools.partial(kernel, sizes + (half,)),
        out_shape=(
            jax.ShapeDtypeStruct((8, 8, batch), f32),
            jax.ShapeDtypeStruct((mp, batch), f32),
        ),
        in_specs=[vmem] * 9,
        out_specs=(vmem, vmem),
        scratch_shapes=[
            V((Z, X, Y, 2, 2) + block, bf16),
            V((modes, 64), bf16),
            V((3, 16, 8, batch), f32),
            V((3, 12, 8, batch), f32),
            V((16 * 80, batch), bf16),
            V((448, 14 * batch), bf16),
            V((384, 12 * batch), bf16),
            V((320, 10 * batch), bf16),
            V((12, 8, batch), f32),
            V((Z, X, Y, 2) + block, f32),
            V((Z, X, Y, 2) + block, bf16),
            V((Z, X, Y, 2) + block, bf16),
            V((1, Z, X, Y, 2) + block, bf16),
            V((1, 8, 128), f32),
            V((Y - 1, Z, X) + block, bf16),
            V((1, 8, 128), f32),
            V((X - 1, Z, Y) + block, bf16),
            V((Z, X) + block, f32),
            V((Z, Y) + block, f32),
            V((Z, X) + block, bf16),
            V((X - 1, Z) + block, bf16),
            V((Z, Y) + block, bf16),
            V((Y - 1, Z) + block, bf16),
            V((Z, 2) + block, bf16),
            V((Z - 1, 2) + block, bf16),
            pltpu.SemaphoreType.DMA((gathers,)),
            pltpu.SemaphoreType.DMA((gathers,)),
            pltpu.SemaphoreType.DMA((16,)),
            pltpu.SemaphoreType.DMA((16,)),
            pltpu.SemaphoreType.DMA((gathers,)),
            pltpu.SemaphoreType.DMA((gathers,)),
        ],
        compiler_params=pltpu.CompilerParams(
            collective_id=0, has_side_effects=True, vmem_limit_bytes=56 * 1024 * 1024
        ),
    )(
        coeffs, flat, observed, first, ahead, back, last,
        jnp.tile(b_two, 12)[:, None], jnp.tile(read_w, 12)[:, None],
    )
    return pressure, grad[:own]


def solution(mesh):
    R, N = mesh.shape["row"], mesh.shape["col"]
    X = 1 << ((R.bit_length() - 1) // 2)
    sizes = (R, N, R // X, X, N // 2)
    return jax.shard_map(
        functools.partial(shards, sizes),
        mesh=mesh,
        in_specs=(
            P(("row", "col"), None),
            P("row", "col", None),
            P("row", "col", None),
            P(),
            P(),
            P(),
            P(),
            P(),
            P(),
            P(),
        ),
        out_specs=(P("row", "col", None), P(("row", "col"), None)),
        check_vma=False,
    )
```

```python
import functools

import jax
import jax.numpy as jnp
from jax import lax
from jax.experimental import pallas as pl
from jax.experimental.pallas import tpu as pltpu
from jax.sharding import PartitionSpec as P

prior_weight = 0.1
MESH = pl.DeviceIdType.MESH
bf16 = jnp.bfloat16
f32 = jnp.float32


def column(vec):
    shape = (32, 32)
    same = lax.broadcasted_iota(jnp.int32, shape, 0) == lax.broadcasted_iota(jnp.int32, shape, 1)
    row = jnp.broadcast_to(vec[...].reshape(1, 32), shape)
    return jnp.sum(jnp.where(same, row, 0.0), axis=1, keepdims=True)


def build_weights(
    lift_w, lift_b, w_one, b_one, w_two, b_two, read_w, first, ahead, back, last, bias_two, read
):
    def iota(shape, axis):
        return lax.broadcasted_iota(jnp.int32, shape, axis)

    def wide(col):
        return jnp.broadcast_to(col[None], (12, 32, 128)).reshape(384, 128)

    bias_two[...] = wide(column(b_two))
    read[...] = wide(column(read_w))
    lw, lb, bias = column(lift_w), column(lift_b), column(b_one)
    lw, lb = jnp.concatenate([lw] * 9, axis=0), jnp.concatenate([lb] * 9, axis=0)
    one = w_one[...].astype(f32)
    r, lane = iota((288, 240), 0), iota((288, 240), 1)
    p = (r >= 96).astype(jnp.int32) + (r >= 192).astype(jnp.int32)
    at = lane - (80 * p + ((r - 96 * p) >> 5) + 4)
    hi = bias.astype(bf16).astype(f32)
    lane = iota((32, 240), 1)
    bias = jnp.where(lane == 72, hi, jnp.where(lane == 73, bias - hi, 0.0))
    for y in range(14):
        spread = jnp.where(
            (at == y) | (at == y + 24), lw, jnp.where(at == y + 48, lb, 0.0)
        )
        block = lax.dot_general(
            one, spread, (((0,), (0,)), ((), ())), precision=lax.Precision.HIGHEST,
            preferred_element_type=f32,
        )
        first[y * 32 : y * 32 + 32, :] = (block + bias).astype(bf16)

    for k in range(3):
        rows = w_two[k * 96 : k * 96 + 96, :]
        for y in range(4):
            move = jnp.where(iota((96, 192), 1) == iota((96, 192), 0) + 32 * y, 1.0, 0.0)
            ahead[k, y * 32 : y * 32 + 32, :] = lax.dot_general(
                rows, move.astype(bf16), (((0,), (0,)), ((), ())), preferred_element_type=f32
            ).astype(bf16)
        rows = w_two[(2 - k) * 96 : (2 - k) * 96 + 96, :]
        moved = []
        for n in range(6):
            move = jnp.where(iota((32, 192), 1) == iota((32, 192), 0) + 32 * n, 1.0, 0.0)
            moved.append(jnp.dot(rows, move.astype(bf16), preferred_element_type=f32))
        for y in range(4):
            back[k, y * 32 : y * 32 + 32, :] = sum(
                moved[y + q][(2 - q) * 32 : (2 - q) * 32 + 32] for q in range(3)
            ).astype(bf16)

    tile = jnp.where((iota((32, 320), 1) & 31) == iota((32, 320), 0), 1.0, 0.0).astype(bf16)
    tiled = jnp.dot(w_one[...], tile, preferred_element_type=f32)
    lane = iota((8, 320), 1) >> 5
    cell = iota((8, 320), 0)
    weighted = tiled * lw
    for k in range(3):
        out = jnp.zeros((8, 320), f32)
        for q in range(3):
            n = (2 - k) * 3 + 2 - q
            taps = jnp.sum(weighted[n * 32 : n * 32 + 32], axis=0, keepdims=True)
            out = out + jnp.where(lane == cell + q, taps, 0.0)
        last[8 * k : 8 * k + 8, :] = out


def kernel(
    sizes, coeffs, basis_hbm, observed, lift_w, lift_b, w_one, b_one, w_two, b_two, read_w,
    pressure, grad,
    basis, first, ahead, back, last, bias_two, read, basis_sem,
    gath, turned, field, obs, stack, hid, gtwo, gone, press_ext, own, own_half,
    away, away_in, a_in, b_in, a_sum, b_sum, c_send, c_in, d_send, d_in,
    z_send, z_in,
    g_ss, g_rs, h_ss, h_rs, r_ss, r_rs,
):
    R, N, Z, X, Y, half = sizes
    row, col = lax.axis_index("row"), lax.axis_index("col")
    z, x = row // X, row % X
    y, c = col // 2, col % 2
    mp = 2 * half
    cells, modes = basis.shape

    fetch = pltpu.make_async_copy(basis_hbm, basis, basis_sem)
    fetch.start()

    z_to = [((lax.rem(z + k, Z) * X + x, col), lax.rem(z + k, Z)) for k in range(1, Z)]
    x_to = [((z * X + lax.rem(x + k, X), col), lax.rem(x + k, X)) for k in range(1, X)]
    y_to = [((row, lax.rem(y + k, Y) * 2 + c), lax.rem(y + k, Y)) for k in range(1, Y)]
    c_to = (row, y * 2 + 1 - c)
    sides = [(dx, dy) for dx in (-1, 0, 1) for dy in (-1, 0, 1) if (dx, dy) != (0, 0)]

    def exists(dx, dy):
        return (row + dx >= 0) & (row + dx < R) & (col + dy >= 0) & (col + dy < N)

    field[...] = jnp.zeros(field.shape, f32)
    obs[...] = jnp.zeros(obs.shape, f32)

    barrier = pltpu.get_barrier_semaphore()
    expect = (Z - 1) + (X - 1) + (Y - 1) + 1
    for dev in [d for d, _ in z_to + x_to + y_to] + [c_to]:
        pl.semaphore_signal(barrier, inc=1, device_id=dev, device_id_type=MESH)
    for dx, dy in sides:
        there = exists(dx, dy)

        @pl.when(there)
        def _():
            pl.semaphore_signal(
                barrier, inc=1, device_id=(row + dx, col + dy), device_id_type=MESH
            )

        expect = expect + there.astype(jnp.int32)
    gath[z, x, y, c] = coeffs[...].reshape(2, half, 128).astype(bf16)
    pl.semaphore_wait(barrier, expect)

    def push(src, dst, ss, rs, dev):
        copy = pltpu.make_async_remote_copy(
            src_ref=src, dst_ref=dst, send_sem=ss, recv_sem=rs, device_id=dev,
            device_id_type=MESH,
        )
        copy.start()
        return copy

    sent = []
    n_gath = [0]

    def spread(ref, peers):
        made = []
        for dev, _ in peers:
            k = n_gath[0]
            n_gath[0] += 1
            made.append(push(ref, ref, g_ss.at[k], g_rs.at[k], dev))
        sent.extend(made)
        return made

    def rim(buf, tile, width, base):
        def parts(dx, dy):
            src = tile if dx == 0 else (
                tile.at[pl.ds(0, width)] if dx < 0 else tile.at[pl.ds(8 - width, width)]
            )
            at = pl.ds(width, 8) if dx == 0 else (
                pl.ds(8 + width, width) if dx < 0 else pl.ds(0, width)
            )
            return src, buf.at[1 - dy, at]

        def do(k, dx, dy):
            src, dst = parts(dx, dy)
            return pltpu.make_async_remote_copy(
                src_ref=src, dst_ref=dst, send_sem=h_ss.at[base + k],
                recv_sem=h_rs.at[base + k], device_id=(row + dx, col + dy),
                device_id_type=MESH,
            )

        def start():
            for k, (dx, dy) in enumerate(sides):
                @pl.when(exists(dx, dy))
                def _():
                    do(k, dx, dy).start()

        def wait_in():
            for k, (dx, dy) in enumerate(sides):
                @pl.when(exists(-dx, -dy))
                def _():
                    do(k, dx, dy).wait_recv()

        def wait_out():
            for k, (dx, dy) in enumerate(sides):
                @pl.when(exists(dx, dy))
                def _():
                    do(k, dx, dy).wait_send()

        return start, wait_in, wait_out

    stage = spread(gath.at[z, x, y, c], z_to)
    obs_start, obs_in, obs_out = rim(obs, observed, 2, 0)
    obs_start()
    obs[1, 2:10] = observed[...]

    build_weights(
        lift_w, lift_b, w_one, b_one, w_two, b_two, read_w,
        first, ahead, back, last, bias_two, read,
    )
    fetch.wait()

    @pl.loop(0, modes // 512)
    def _(i):
        at = pl.multiple_of(i * 512, 512)
        turned[pl.ds(at, 512), :] = basis[:, pl.ds(at, 512)].T.astype(bf16)

    for copy in stage:
        copy.wait_recv()
    stage_a = spread(gath.at[:, x, y, c, 0], x_to)
    stage_b = spread(gath.at[:, x, y, c, 1], y_to)
    for copy in stage_a:
        copy.wait_recv()
    stage_a = spread(gath.at[:, :, y, c, 0], y_to)
    for copy in stage_b:
        copy.wait_recv()
    stage_b = spread(gath.at[:, x, :, c, 1], x_to)
    for copy in stage_a + stage_b:
        copy.wait_recv()
    stage = spread(gath.at[:, :, :, c], [(c_to, None)])
    for copy in stage:
        copy.wait_recv()

    group = X * Y * 2

    own_field = jnp.zeros((cells, 128), f32)
    for iz in range(Z):
        block = gath[iz].reshape(group * mp, 128)
        own_field = own_field + jnp.dot(
            basis[:, iz * group * mp : (iz + 1) * group * mp].astype(bf16), block,
            preferred_element_type=f32,
        )
    tile = press_ext.at[pl.ds(0, 8)]
    press_ext[0:8] = own_field.reshape(8, 8, 128)
    field[1, 4:12] = own_field.reshape(8, 8, 128)
    field_start, field_in, field_out = rim(field, tile, 4, 8)
    field_start()
    field_in()
    obs_in()
    field_out()
    obs_out()

    ones = jnp.ones((8, 128), f32)
    y_at = lax.broadcasted_iota(jnp.int32, (24, 128), 0) + (col * 8 - 8)
    y_in = (y_at >= 0) & (y_at < N * 8)

    @pl.loop(0, 16)
    def _(i):
        values = jnp.concatenate([field[0, i], field[1, i], field[2, i]], axis=0)
        hi = values.astype(bf16).astype(f32)
        xg = row * 8 + i - 4
        inside = jnp.where(y_in & (xg >= 0) & (xg < R * 8), 1.0, 0.0)
        full = jnp.concatenate([hi, values - hi, inside, ones], axis=0)
        stack[pl.ds(pl.multiple_of(i * 80, 16), 80), :] = full.astype(bf16)

    def inside(count, off, xg):
        at = lax.broadcasted_iota(jnp.int32, (count * 32, 128), 0)
        low = (off - col * 8) * 32
        high = jnp.where((xg >= 0) & (xg < R * 8), low + N * 256, -1)
        return (at >= low) & (at < high)

    @pl.loop(0, 14)
    def _(i):
        rows = stack[pl.ds(pl.multiple_of(i * 80, 16), 240), :]
        acc = jnp.dot(first[...], rows, preferred_element_type=f32)
        value = jnp.where(inside(14, 3, row * 8 + i - 3), jnp.tanh(acc), 0.0)
        hid[:, pl.ds(pl.multiple_of(i * 128, 128), 128)] = value.astype(bf16)

    def conv(w, src, starts, at):
        out = []
        for s in starts:
            acc = None
            for k in range(3):
                v = src[s * 32 : s * 32 + 192, pl.ds(pl.multiple_of(at + k * 128, 128), 256)]
                d = jnp.dot(w[k], v, preferred_element_type=f32)
                acc = d if acc is None else acc + d
            out.append(acc)
        return out

    @pl.loop(0, 6)
    def _(i):
        at = i * 256
        acc = jnp.concatenate(conv(ahead, hid, (0, 4, 8), at), axis=0)
        for s in range(2):
            xi = i * 2 + s
            t = jnp.tanh(acc[:, s * 128 : s * 128 + 128] + bias_two[...])
            pr = jnp.sum((t * read[...]).reshape(12, 32, 128), axis=1)
            seen = jnp.concatenate([obs[0, xi], obs[1, xi], obs[2, xi]], axis=0)[6:18]
            miss = jnp.broadcast_to((pr - seen)[:, None, :], (12, 32, 128)).reshape(384, 128)
            g = miss * read[...] * (1.0 - t * t)
            g = jnp.where(inside(12, 2, row * 8 + xi - 2), g, 0.0)
            gtwo[:, pl.ds(pl.multiple_of(at + s * 128, 128), 128)] = g.astype(bf16)
            press_ext[xi] = pr[2:10]

    pressure[...] = press_ext[2:10]

    @pl.loop(0, 5)
    def _(i):
        at = i * 256
        a0, a1, a2 = conv(back, gtwo, (0, 4, 6), at)
        acc = jnp.concatenate([a0, a1, a2[64:]], axis=0)
        for s in range(2):
            xi = i * 2 + s
            h = hid[64:384, pl.ds(pl.multiple_of(at + (2 + s) * 128, 128), 128)].astype(f32)
            g = acc[:, s * 128 : s * 128 + 128] * (1.0 - h * h)
            g = jnp.where(inside(10, 1, row * 8 + xi - 1), g, 0.0)
            gone[:, pl.ds(pl.multiple_of(at + s * 128, 128), 128)] = g.astype(bf16)

    parts = jnp.dot(last[...].astype(bf16), gone[...], preferred_element_type=f32)
    slabs = [
        sum(parts[8 * k : 8 * k + 8, (xi + k) * 128 : (xi + k + 1) * 128] for k in range(3))
        for xi in range(8)
    ]
    grad_field = jnp.concatenate(slabs, axis=0).astype(bf16)

    def project(core, into, kind):
        @pl.loop(0, Z * X * Y)
        def _(j):
            at = pl.multiple_of((j * 2 + core) * mp, mp)
            d = jnp.dot(turned[pl.ds(at, mp), :], grad_field, preferred_element_type=f32)
            jz, jr = j // (X * Y), j % (X * Y)
            into[jz, jr // Y, jr % Y] = d.reshape(2, half, 128).astype(kind)

    n_red = [0]

    def shed(src_at, slots, peers):
        made = []
        for k, (dev, peer) in enumerate(peers):
            i = n_red[0]
            n_red[0] += 1
            made.append(push(src_at(peer), slots.at[k], r_ss.at[i], r_rs.at[i], dev))
        sent.extend(made)
        return made

    project(1 - c, away, bf16)
    stage = shed(lambda _: away, away_in, [(c_to, None)])
    project(c, own, f32)
    for copy in stage:
        copy.wait_recv()
    own[...] = own[...] + away_in[0].astype(f32)
    own_half[...] = own[...].astype(bf16)
    stage_a = shed(lambda p: own_half.at[:, :, p, 0], a_in, y_to)
    stage_b = shed(lambda p: own_half.at[:, p, :, 1], b_in, x_to)
    for copy in stage_a:
        copy.wait_recv()
    total = own[:, :, y, 0]
    for k in range(Y - 1):
        total = total + a_in[k].astype(f32)
    a_sum[...] = total
    c_send[...] = total.astype(bf16)
    stage_a = shed(lambda p: c_send.at[:, p], c_in, x_to)
    for copy in stage_b:
        copy.wait_recv()
    total = own[:, x, :, 1]
    for k in range(X - 1):
        total = total + b_in[k].astype(f32)
    b_sum[...] = total
    d_send[...] = total.astype(bf16)
    stage_b = shed(lambda p: d_send.at[:, p], d_in, y_to)
    for copy in stage_a + stage_b:
        copy.wait_recv()
    part_a, part_b = a_sum[:, x], b_sum[:, y]
    for k in range(X - 1):
        part_a = part_a + c_in[k].astype(f32)
    for k in range(Y - 1):
        part_b = part_b + d_in[k].astype(f32)
    own[:, 0, 0, 0] = part_a
    own[:, 0, 0, 1] = part_b
    z_send[:, 0] = part_a.astype(bf16)
    z_send[:, 1] = part_b.astype(bf16)
    stage = shed(lambda p: z_send.at[p], z_in, z_to)
    for copy in stage:
        copy.wait_recv()
    total = own[z, 0, 0]
    for k in range(Z - 1):
        total = total + z_in[k].astype(f32)
    grad[...] = total.reshape(mp, 128) + prior_weight * coeffs[...]
    for copy in sent:
        copy.wait_send()


def shards(sizes, coeffs, basis, observed, lift_w, lift_b, w_one, b_one, w_two, b_two, read_w):
    R, N, Z, X, Y = sizes
    mode_count, batch = basis.shape[2], coeffs.shape[1]
    own = coeffs.shape[0]
    mp = max(own, 32)
    half = mp // 2
    flat = basis.reshape(64, mode_count)
    if mp != own:
        flat = jnp.pad(flat.reshape(64, R * N, own), ((0, 0), (0, 0), (0, mp - own)))
        flat = flat.reshape(64, R * N * mp)
        coeffs = jnp.pad(coeffs, ((0, mp - own), (0, 0)))
    modes = R * N * mp
    vmem = pl.BlockSpec(memory_space=pltpu.VMEM)
    block = (half, batch)
    gathers = (Z - 1) + 2 * (X - 1) + 2 * (Y - 1) + 1
    V = pltpu.VMEM
    pressure, grad = pl.pallas_call(
        functools.partial(kernel, sizes + (half,)),
        out_shape=(
            jax.ShapeDtypeStruct((8, 8, batch), f32),
            jax.ShapeDtypeStruct((mp, batch), f32),
        ),
        in_specs=[vmem, pl.BlockSpec(memory_space=pl.ANY)] + [vmem] * 8,
        out_specs=(vmem, vmem),
        scratch_shapes=[
            V((64, modes), f32),
            V((448, 240), bf16),
            V((3, 128, 192), bf16),
            V((3, 128, 192), bf16),
            V((24, 320), f32),
            V((384, 128), f32),
            V((384, 128), f32),
            pltpu.SemaphoreType.DMA,
            V((Z, X, Y, 2, 2) + block, bf16),
            V((modes, 64), bf16),
            V((3, 16, 8, batch), f32),
            V((3, 12, 8, batch), f32),
            V((16 * 80, batch), bf16),
            V((448, 14 * batch), bf16),
            V((384, 12 * batch), bf16),
            V((320, 10 * batch), bf16),
            V((12, 8, batch), f32),
            V((Z, X, Y, 2) + block, f32),
            V((Z, X, Y, 2) + block, bf16),
            V((Z, X, Y, 2) + block, bf16),
            V((1, Z, X, Y, 2) + block, bf16),
            V((Y - 1, Z, X) + block, bf16),
            V((X - 1, Z, Y) + block, bf16),
            V((Z, X) + block, f32),
            V((Z, Y) + block, f32),
            V((Z, X) + block, bf16),
            V((X - 1, Z) + block, bf16),
            V((Z, Y) + block, bf16),
            V((Y - 1, Z) + block, bf16),
            V((Z, 2) + block, bf16),
            V((Z - 1, 2) + block, bf16),
            pltpu.SemaphoreType.DMA((gathers,)),
            pltpu.SemaphoreType.DMA((gathers,)),
            pltpu.SemaphoreType.DMA((16,)),
            pltpu.SemaphoreType.DMA((16,)),
            pltpu.SemaphoreType.DMA((gathers,)),
            pltpu.SemaphoreType.DMA((gathers,)),
        ],
        compiler_params=pltpu.CompilerParams(
            collective_id=0, has_side_effects=True, vmem_limit_bytes=56 * 1024 * 1024
        ),
    )(
        coeffs, flat, observed, lift_w, lift_b, w_one.reshape(288, 32), b_one,
        w_two.reshape(288, 32), b_two, read_w,
    )
    return pressure, grad[:own]


def solution(mesh):
    R, N = mesh.shape["row"], mesh.shape["col"]
    X = 1 << ((R.bit_length() - 1) // 2)
    sizes = (R, N, R // X, X, N // 2)
    return jax.shard_map(
        functools.partial(shards, sizes),
        mesh=mesh,
        in_specs=(
            P(("row", "col"), None),
            P("row", "col", None),
            P("row", "col", None),
            P(),
            P(),
            P(),
            P(),
            P(),
            P(),
            P(),
        ),
        out_specs=(P("row", "col", None), P(("row", "col"), None)),
        check_vma=False,
    )
```

```python
import functools

import jax
import jax.numpy as jnp
from jax import lax
from jax.experimental import pallas as pl
from jax.experimental.pallas import tpu as pltpu
from jax.sharding import PartitionSpec as P

prior_weight = 0.1
MESH = pl.DeviceIdType.MESH
bf16 = jnp.bfloat16
f32 = jnp.float32


def column(vec):
    shape = (32, 32)
    same = lax.broadcasted_iota(jnp.int32, shape, 0) == lax.broadcasted_iota(jnp.int32, shape, 1)
    row = jnp.broadcast_to(vec[...].reshape(1, 32), shape)
    return jnp.sum(jnp.where(same, row, 0.0), axis=1, keepdims=True)


def iota(shape, axis):
    return lax.broadcasted_iota(jnp.int32, shape, axis)


def build_first(lift_w, lift_b, w_one, b_one, b_two, read_w, first, bias_two, read):

    def wide(col):
        return jnp.broadcast_to(col[None], (12, 32, 128)).reshape(384, 128)

    bias_two[...] = wide(column(b_two))
    read[...] = wide(column(read_w))
    lw, lb, bias = column(lift_w), column(lift_b), column(b_one)
    lw, lb = jnp.concatenate([lw] * 9, axis=0), jnp.concatenate([lb] * 9, axis=0)
    one = w_one[...].astype(f32)
    r, lane = iota((288, 240), 0), iota((288, 240), 1)
    p = (r >= 96).astype(jnp.int32) + (r >= 192).astype(jnp.int32)
    at = lane - (80 * p + ((r - 96 * p) >> 5) + 4)
    hi = bias.astype(bf16).astype(f32)
    lane = iota((32, 240), 1)
    bias = jnp.where(lane == 72, hi, jnp.where(lane == 73, bias - hi, 0.0))
    for y in range(14):
        spread = jnp.where(
            (at == y) | (at == y + 24), lw, jnp.where(at == y + 48, lb, 0.0)
        )
        block = lax.dot_general(
            one, spread, (((0,), (0,)), ((), ())), precision=lax.Precision.HIGHEST,
            preferred_element_type=f32,
        )
        first[y * 32 : y * 32 + 32, :] = (block + bias).astype(bf16)


def build_others(lift_w, w_one, w_two, ahead, back, last):
    lw = jnp.concatenate([column(lift_w)] * 9, axis=0)
    for k in range(3):
        rows = w_two[k * 96 : k * 96 + 96, :]
        for y in range(4):
            move = jnp.where(iota((96, 192), 1) == iota((96, 192), 0) + 32 * y, 1.0, 0.0)
            ahead[k, y * 32 : y * 32 + 32, :] = lax.dot_general(
                rows, move.astype(bf16), (((0,), (0,)), ((), ())), preferred_element_type=f32
            ).astype(bf16)
        rows = w_two[(2 - k) * 96 : (2 - k) * 96 + 96, :]
        moved = []
        for n in range(6):
            move = jnp.where(iota((32, 192), 1) == iota((32, 192), 0) + 32 * n, 1.0, 0.0)
            moved.append(jnp.dot(rows, move.astype(bf16), preferred_element_type=f32))
        for y in range(4):
            back[k, y * 32 : y * 32 + 32, :] = sum(
                moved[y + q][(2 - q) * 32 : (2 - q) * 32 + 32] for q in range(3)
            ).astype(bf16)

    tile = jnp.where((iota((32, 320), 1) & 31) == iota((32, 320), 0), 1.0, 0.0).astype(bf16)
    tiled = jnp.dot(w_one[...], tile, preferred_element_type=f32)
    lane = iota((8, 320), 1) >> 5
    cell = iota((8, 320), 0)
    weighted = tiled * lw
    for k in range(3):
        out = jnp.zeros((8, 320), f32)
        for q in range(3):
            n = (2 - k) * 3 + 2 - q
            taps = jnp.sum(weighted[n * 32 : n * 32 + 32], axis=0, keepdims=True)
            out = out + jnp.where(lane == cell + q, taps, 0.0)
        last[8 * k : 8 * k + 8, :] = out


def kernel(
    sizes, *refs,
):
    given, refs = refs[:10], refs[10:]
    (
        pressure_out, grad_out,
        coeffs, basis, observed_own, lift_w, lift_b, w_one, b_one, w_two, b_two, read_w,
        pressure, grad, in_sem, out_sem,
        first, ahead, back, last, bias_two, read,
        gath, turned, basis_half, field, obs, stack, hid, gtwo, gone, press_ext, own, own_half,
        away, away_in, a_in, b_in, a_sum, b_sum, c_send, c_in, d_send, d_in, z_send, z_in,
        g_ss, g_rs, h_ss, h_rs, r_ss, r_rs,
    ) = refs
    R, N, Z, X, Y, half = sizes
    row, col = lax.axis_index("row"), lax.axis_index("col")
    z, x = row // X, row % X
    y, c = col // 2, col % 2
    mp = 2 * half
    cells, modes = basis.shape

    local = (coeffs, basis, observed_own, lift_w, lift_b, w_one, b_one, w_two, b_two, read_w)
    fetch = [
        pltpu.make_async_copy(src, dst, in_sem.at[k]) for k, (src, dst) in enumerate(zip(given, local))
    ]
    for k in (0, 2, 3, 4, 5, 6, 7, 8, 9, 1):
        fetch[k].start()

    z_to = [((lax.rem(z + k, Z) * X + x, col), lax.rem(z + k, Z)) for k in range(1, Z)]
    x_to = [((z * X + lax.rem(x + k, X), col), lax.rem(x + k, X)) for k in range(1, X)]
    y_to = [((row, lax.rem(y + k, Y) * 2 + c), lax.rem(y + k, Y)) for k in range(1, Y)]
    c_to = (row, y * 2 + 1 - c)
    sides = [(dx, dy) for dx in (-1, 0, 1) for dy in (-1, 0, 1) if (dx, dy) != (0, 0)]

    def exists(dx, dy):
        return (row + dx >= 0) & (row + dx < R) & (col + dy >= 0) & (col + dy < N)

    field[...] = jnp.zeros(field.shape, f32)
    obs[...] = jnp.zeros(obs.shape, f32)

    barrier = pltpu.get_barrier_semaphore()
    expect = (Z - 1) + (X - 1) + (Y - 1) + 1
    for dev in [d for d, _ in z_to + x_to + y_to] + [c_to]:
        pl.semaphore_signal(barrier, inc=1, device_id=dev, device_id_type=MESH)
    for dx, dy in sides:
        there = exists(dx, dy)

        @pl.when(there)
        def _():
            pl.semaphore_signal(
                barrier, inc=1, device_id=(row + dx, col + dy), device_id_type=MESH
            )

        expect = expect + there.astype(jnp.int32)
    fetch[0].wait()
    gath[z, x, y, c] = coeffs[...].reshape(2, half, 128).astype(bf16)
    pl.semaphore_wait(barrier, expect)

    def push(src, dst, ss, rs, dev):
        copy = pltpu.make_async_remote_copy(
            src_ref=src, dst_ref=dst, send_sem=ss, recv_sem=rs, device_id=dev,
            device_id_type=MESH,
        )
        copy.start()
        return copy

    sent = []
    n_gath = [0]

    def spread(ref, peers):
        made = []
        for dev, _ in peers:
            k = n_gath[0]
            n_gath[0] += 1
            made.append(push(ref, ref, g_ss.at[k], g_rs.at[k], dev))
        sent.extend(made)
        return made

    def rim(buf, width, base):
        def parts(dx, dy):
            src = buf.at[1, pl.ds(width, 8)] if dx == 0 else (
                buf.at[1, pl.ds(width, width)] if dx < 0 else buf.at[1, pl.ds(8, width)]
            )
            at = pl.ds(width, 8) if dx == 0 else (
                pl.ds(8 + width, width) if dx < 0 else pl.ds(0, width)
            )
            return src, buf.at[1 - dy, at]

        def do(k, dx, dy):
            src, dst = parts(dx, dy)
            return pltpu.make_async_remote_copy(
                src_ref=src, dst_ref=dst, send_sem=h_ss.at[base + k],
                recv_sem=h_rs.at[base + k], device_id=(row + dx, col + dy),
                device_id_type=MESH,
            )

        def start():
            for k, (dx, dy) in enumerate(sides):
                @pl.when(exists(dx, dy))
                def _():
                    do(k, dx, dy).start()

        def wait_in():
            for k, (dx, dy) in enumerate(sides):
                @pl.when(exists(-dx, -dy))
                def _():
                    do(k, dx, dy).wait_recv()

        def wait_out():
            for k, (dx, dy) in enumerate(sides):
                @pl.when(exists(dx, dy))
                def _():
                    do(k, dx, dy).wait_send()

        return start, wait_in, wait_out

    came = [lax.rem(z - k + Z, Z) for k in range(Z)]
    stage = spread(gath.at[z, x, y, c], z_to)

    def once(k):
        at = came[k]
        return (spread(gath.at[at, x, y, c, 0], x_to), spread(gath.at[at, x, y, c, 1], y_to))

    def twice(k, made):
        at = came[k]
        for copy in made[0]:
            copy.wait_recv()
        to_y = spread(gath.at[at, :, y, c, 0], y_to)
        for copy in made[1]:
            copy.wait_recv()
        return to_y + spread(gath.at[at, x, :, c, 1], x_to)

    moving = [once(0)]
    fetch[2].wait()
    obs[1, 2:10] = observed_own[...]
    obs_start, obs_in, obs_out = rim(obs, 2, 0)
    obs_start()
    for k in range(3, 10):
        fetch[k].wait()
    build_first(lift_w, lift_b, w_one, b_one, b_two, read_w, first, bias_two, read)
    for k in range(1, Z):
        stage[k - 1].wait_recv()
        moving.append(once(k))
    moving = [twice(k, made) for k, made in enumerate(moving)]
    build_others(lift_w, w_one, w_two, ahead, back, last)
    fetch[1].wait()

    def arrange(i):
        at = pl.multiple_of(i * 512, 512)
        part = basis[:, pl.ds(at, 512)]
        basis_half[:, pl.ds(at, 512)] = part.astype(bf16)
        turned[pl.ds(at, 512), :] = part.T.astype(bf16)

    done = []
    for k, made in enumerate(moving):
        for copy in made:
            copy.wait_recv()
        done.extend(spread(gath.at[came[k], :, :, c], [(c_to, None)]))
        if k == 0:
            pl.loop(0, modes // 512)(arrange)

    group = X * Y * 2 * mp
    own_field = jnp.zeros((cells, 128), f32)
    for k, copy in enumerate(done):
        copy.wait_recv()
        own_field = own_field + jnp.dot(
            basis_half[:, pl.ds(pl.multiple_of(came[k] * group, 128), group)],
            gath[came[k]].reshape(group, 128), preferred_element_type=f32,
        )
    field[1, 4:12] = own_field.reshape(8, 8, 128)
    field_start, field_in, field_out = rim(field, 4, 8)
    field_start()
    field_in()
    obs_in()
    field_out()
    obs_out()

    ones = jnp.ones((8, 128), f32)
    y_at = lax.broadcasted_iota(jnp.int32, (24, 128), 0) + (col * 8 - 8)
    y_in = (y_at >= 0) & (y_at < N * 8)

    @pl.loop(0, 16, unroll=2)
    def _(i):
        values = jnp.concatenate([field[0, i], field[1, i], field[2, i]], axis=0)
        hi = values.astype(bf16).astype(f32)
        xg = row * 8 + i - 4
        inside = jnp.where(y_in & (xg >= 0) & (xg < R * 8), 1.0, 0.0)
        full = jnp.concatenate([hi, values - hi, inside, ones], axis=0)
        stack[pl.ds(pl.multiple_of(i * 80, 16), 80), :] = full.astype(bf16)

    def inside(count, off, xg):
        at = lax.broadcasted_iota(jnp.int32, (count * 32, 128), 0)
        low = (off - col * 8) * 32
        high = jnp.where((xg >= 0) & (xg < R * 8), low + N * 256, -1)
        return (at >= low) & (at < high)

    @pl.loop(0, 14, unroll=2)
    def _(i):
        rows = stack[pl.ds(pl.multiple_of(i * 80, 16), 240), :]
        acc = jnp.dot(first[...], rows, preferred_element_type=f32)
        value = jnp.where(inside(14, 3, row * 8 + i - 3), jnp.tanh(acc), 0.0)
        hid[:, pl.ds(pl.multiple_of(i * 128, 128), 128)] = value.astype(bf16)

    def conv(w, src, starts, at):
        out = []
        for s in starts:
            acc = None
            for k in range(3):
                v = src[s * 32 : s * 32 + 192, pl.ds(pl.multiple_of(at + k * 128, 128), 256)]
                d = jnp.dot(w[k], v, preferred_element_type=f32)
                acc = d if acc is None else acc + d
            out.append(acc)
        return out

    @pl.loop(0, 6)
    def _(i):
        at = i * 256
        acc = jnp.concatenate(conv(ahead, hid, (0, 4, 8), at), axis=0)
        for s in range(2):
            xi = i * 2 + s
            t = jnp.tanh(acc[:, s * 128 : s * 128 + 128] + bias_two[...])
            pr = jnp.sum((t * read[...]).reshape(12, 32, 128), axis=1)
            seen = jnp.concatenate([obs[0, xi], obs[1, xi], obs[2, xi]], axis=0)[6:18]
            miss = jnp.broadcast_to((pr - seen)[:, None, :], (12, 32, 128)).reshape(384, 128)
            g = miss * read[...] * (1.0 - t * t)
            g = jnp.where(inside(12, 2, row * 8 + xi - 2), g, 0.0)
            gtwo[:, pl.ds(pl.multiple_of(at + s * 128, 128), 128)] = g.astype(bf16)
            press_ext[xi] = pr[2:10]

    pressure[...] = press_ext[2:10].reshape(64, 128)
    pressure_copy = pltpu.make_async_copy(pressure, pressure_out, out_sem.at[0])
    pressure_copy.start()

    @pl.loop(0, 5)
    def _(i):
        at = i * 256
        a0, a1, a2 = conv(back, gtwo, (0, 4, 6), at)
        acc = jnp.concatenate([a0, a1, a2[64:]], axis=0)
        for s in range(2):
            xi = i * 2 + s
            h = hid[64:384, pl.ds(pl.multiple_of(at + (2 + s) * 128, 128), 128)].astype(f32)
            g = acc[:, s * 128 : s * 128 + 128] * (1.0 - h * h)
            g = jnp.where(inside(10, 1, row * 8 + xi - 1), g, 0.0)
            gone[:, pl.ds(pl.multiple_of(at + s * 128, 128), 128)] = g.astype(bf16)

    parts = jnp.dot(last[...].astype(bf16), gone[...], preferred_element_type=f32)
    slabs = [
        sum(parts[8 * k : 8 * k + 8, (xi + k) * 128 : (xi + k + 1) * 128] for k in range(3))
        for xi in range(8)
    ]
    grad_field = jnp.concatenate(slabs, axis=0).astype(bf16)

    def project(core, at, into, kind):
        @pl.loop(0, X * Y, unroll=4)
        def _(j):
            rows = pl.multiple_of(((at * X * Y + j) * 2 + core) * mp, mp)
            d = jnp.dot(turned[pl.ds(rows, mp), :], grad_field, preferred_element_type=f32)
            into[at, j // Y, j % Y] = d.reshape(2, half, 128).astype(kind)

    n_red = [0]

    def shed(pairs):
        made = []
        for src, dst, dev in pairs:
            i = n_red[0]
            n_red[0] += 1
            made.append(push(src, dst, r_ss.at[i], r_rs.at[i], dev))
        sent.extend(made)
        return made

    order = [lax.rem(z + k + 1, Z) for k in range(Z)]
    moving = []
    for at in order:
        project(1 - c, at, away, bf16)
        moving.append(shed([(away.at[at], away_in.at[at], c_to)]))
    for at in order:
        project(c, at, own, f32)
    both = []
    for at, made in zip(order, moving):
        made[0].wait_recv()
        total = own[at] + away_in[at].astype(f32)
        own[at] = total
        own_half[at] = total.astype(bf16)
        both.append((
            shed([(own_half.at[at, :, p, 0], a_in.at[k, at], d) for k, (d, p) in enumerate(y_to)]),
            shed([(own_half.at[at, p, :, 1], b_in.at[k, at], d) for k, (d, p) in enumerate(x_to)]),
        ))
    moving = []
    for at, (made_a, made_b) in zip(order, both):
        for copy in made_a:
            copy.wait_recv()
        total = own[at, :, y, 0]
        for k in range(Y - 1):
            total = total + a_in[k, at].astype(f32)
        a_sum[at] = total
        c_send[at] = total.astype(bf16)
        made_a = shed([(c_send.at[at, p], c_in.at[k, at], d) for k, (d, p) in enumerate(x_to)])
        for copy in made_b:
            copy.wait_recv()
        total = own[at, x, :, 1]
        for k in range(X - 1):
            total = total + b_in[k, at].astype(f32)
        b_sum[at] = total
        d_send[at] = total.astype(bf16)
        made_b = shed([(d_send.at[at, p], d_in.at[k, at], d) for k, (d, p) in enumerate(y_to)])
        moving.append(made_a + made_b)
    stage = []
    for n, (at, made) in enumerate(zip(order, moving)):
        for copy in made:
            copy.wait_recv()
        part_a, part_b = a_sum[at, x], b_sum[at, y]
        for k in range(X - 1):
            part_a = part_a + c_in[k, at].astype(f32)
        for k in range(Y - 1):
            part_b = part_b + d_in[k, at].astype(f32)
        if n < Z - 1:
            z_send[at, 0] = part_a.astype(bf16)
            z_send[at, 1] = part_b.astype(bf16)
            stage.extend(shed([(z_send.at[at], z_in.at[n], z_to[n][0])]))
    total = jnp.concatenate([part_a, part_b], axis=0) + prior_weight * coeffs[...]
    for k, copy in enumerate(stage):
        copy.wait_recv()
        total = total + z_in[k].astype(f32).reshape(mp, 128)
    grad[...] = total
    grad_copy = pltpu.make_async_copy(grad, grad_out, out_sem.at[1])
    grad_copy.start()
    for copy in sent:
        copy.wait_send()
    pressure_copy.wait()
    grad_copy.wait()


def shards(sizes, coeffs, basis, observed, lift_w, lift_b, w_one, b_one, w_two, b_two, read_w):
    R, N, Z, X, Y = sizes
    mode_count, batch = basis.shape[2], coeffs.shape[1]
    own = coeffs.shape[0]
    mp = max(own, 32)
    half = mp // 2
    flat = basis.reshape(64, mode_count)
    if mp != own:
        flat = jnp.pad(flat.reshape(64, R * N, own), ((0, 0), (0, 0), (0, mp - own)))
        flat = flat.reshape(64, R * N * mp)
        coeffs = jnp.pad(coeffs, ((0, mp - own), (0, 0)))
    modes = R * N * mp
    hbm = pl.BlockSpec(memory_space=pl.ANY)
    block = (half, batch)
    copies = (Z - 1) + Z * (2 * (X - 1) + 2 * (Y - 1) + 1)
    V = pltpu.VMEM
    pressure, grad = pl.pallas_call(
        functools.partial(kernel, sizes + (half,)),
        out_shape=(
            jax.ShapeDtypeStruct((64, batch), f32),
            jax.ShapeDtypeStruct((mp, batch), f32),
        ),
        in_specs=[hbm] * 10,
        out_specs=(hbm, hbm),
        scratch_shapes=[
            V((mp, batch), f32),
            V((64, modes), f32),
            V((8, 8, batch), f32),
            V((32,), f32),
            V((32,), f32),
            V((288, 32), bf16),
            V((32,), f32),
            V((288, 32), bf16),
            V((32,), f32),
            V((32,), f32),
            V((64, batch), f32),
            V((mp, batch), f32),
            pltpu.SemaphoreType.DMA((10,)),
            pltpu.SemaphoreType.DMA((2,)),
            V((448, 240), bf16),
            V((3, 128, 192), bf16),
            V((3, 128, 192), bf16),
            V((24, 320), f32),
            V((384, 128), f32),
            V((384, 128), f32),
            V((Z, X, Y, 2, 2) + block, bf16),
            V((modes, 64), bf16),
            V((64, modes), bf16),
            V((3, 16, 8, batch), f32),
            V((3, 12, 8, batch), f32),
            V((16 * 80, batch), bf16),
            V((448, 14 * batch), bf16),
            V((384, 12 * batch), bf16),
            V((320, 10 * batch), bf16),
            V((12, 8, batch), f32),
            V((Z, X, Y, 2) + block, f32),
            V((Z, X, Y, 2) + block, bf16),
            V((Z, X, Y, 2) + block, bf16),
            V((Z, X, Y, 2) + block, bf16),
            V((Y - 1, Z, X) + block, bf16),
            V((X - 1, Z, Y) + block, bf16),
            V((Z, X) + block, f32),
            V((Z, Y) + block, f32),
            V((Z, X) + block, bf16),
            V((X - 1, Z) + block, bf16),
            V((Z, Y) + block, bf16),
            V((Y - 1, Z) + block, bf16),
            V((Z, 2) + block, bf16),
            V((Z - 1, 2) + block, bf16),
            pltpu.SemaphoreType.DMA((copies,)),
            pltpu.SemaphoreType.DMA((copies,)),
            pltpu.SemaphoreType.DMA((16,)),
            pltpu.SemaphoreType.DMA((16,)),
            pltpu.SemaphoreType.DMA((copies,)),
            pltpu.SemaphoreType.DMA((copies,)),
        ],
        compiler_params=pltpu.CompilerParams(
            collective_id=0, has_side_effects=True, vmem_limit_bytes=56 * 1024 * 1024
        ),
    )(
        coeffs, flat, observed, lift_w, lift_b, w_one.reshape(288, 32), b_one,
        w_two.reshape(288, 32), b_two, read_w,
    )
    return pressure.reshape(8, 8, batch), grad[:own]


def solution(mesh):
    R, N = mesh.shape["row"], mesh.shape["col"]
    X = 1 << ((R.bit_length() - 1) // 2)
    sizes = (R, N, R // X, X, N // 2)
    return jax.shard_map(
        functools.partial(shards, sizes),
        mesh=mesh,
        in_specs=(
            P(("row", "col"), None),
            P("row", "col", None),
            P("row", "col", None),
            P(),
            P(),
            P(),
            P(),
            P(),
            P(),
            P(),
        ),
        out_specs=(P("row", "col", None), P(("row", "col"), None)),
        check_vma=False,
    )
```

```python
import functools

import jax
import jax.numpy as jnp
from jax import lax
from jax.experimental import pallas as pl
from jax.experimental.pallas import tpu as pltpu
from jax.sharding import PartitionSpec as P

prior_weight = 0.1
MESH = pl.DeviceIdType.MESH
bf16 = jnp.bfloat16
f32 = jnp.float32


def column(vec):
    shape = (32, 32)
    same = lax.broadcasted_iota(jnp.int32, shape, 0) == lax.broadcasted_iota(jnp.int32, shape, 1)
    row = jnp.broadcast_to(vec[...].reshape(1, 32), shape)
    return jnp.sum(jnp.where(same, row, 0.0), axis=1, keepdims=True)


def iota(shape, axis):
    return lax.broadcasted_iota(jnp.int32, shape, axis)


def build_first(lift_w, lift_b, w_one, b_one, b_two, read_w, first, bias_two, read):

    def wide(col):
        return jnp.broadcast_to(col[None], (12, 32, 128)).reshape(384, 128)

    bias_two[...] = wide(column(b_two))
    read[...] = wide(column(read_w))
    lw, lb, bias = column(lift_w), column(lift_b), column(b_one)
    lw, lb = jnp.concatenate([lw] * 9, axis=0), jnp.concatenate([lb] * 9, axis=0)
    one = w_one[...].astype(f32)
    r, lane = iota((288, 240), 0), iota((288, 240), 1)
    p = (r >= 96).astype(jnp.int32) + (r >= 192).astype(jnp.int32)
    at = lane - (80 * p + ((r - 96 * p) >> 5) + 4)
    hi = bias.astype(bf16).astype(f32)
    lane = iota((32, 240), 1)
    bias = jnp.where(lane == 72, hi, jnp.where(lane == 73, bias - hi, 0.0))
    for y in range(14):
        spread = jnp.where(
            (at == y) | (at == y + 24), lw, jnp.where(at == y + 48, lb, 0.0)
        )
        block = lax.dot_general(
            one, spread, (((0,), (0,)), ((), ())), precision=lax.Precision.HIGHEST,
            preferred_element_type=f32,
        )
        first[y * 32 : y * 32 + 32, :] = (block + bias).astype(bf16)


def build_others(lift_w, w_one, w_two, ahead, back, last):
    lw = jnp.concatenate([column(lift_w)] * 9, axis=0)
    for k in range(3):
        rows = w_two[k * 96 : k * 96 + 96, :]
        for y in range(4):
            move = jnp.where(iota((96, 192), 1) == iota((96, 192), 0) + 32 * y, 1.0, 0.0)
            ahead[k, y * 32 : y * 32 + 32, :] = lax.dot_general(
                rows, move.astype(bf16), (((0,), (0,)), ((), ())), preferred_element_type=f32
            ).astype(bf16)
        rows = w_two[(2 - k) * 96 : (2 - k) * 96 + 96, :]
        moved = []
        for n in range(6):
            move = jnp.where(iota((32, 192), 1) == iota((32, 192), 0) + 32 * n, 1.0, 0.0)
            moved.append(jnp.dot(rows, move.astype(bf16), preferred_element_type=f32))
        for y in range(4):
            back[k, y * 32 : y * 32 + 32, :] = sum(
                moved[y + q][(2 - q) * 32 : (2 - q) * 32 + 32] for q in range(3)
            ).astype(bf16)

    tile = jnp.where((iota((32, 320), 1) & 31) == iota((32, 320), 0), 1.0, 0.0).astype(bf16)
    tiled = jnp.dot(w_one[...], tile, preferred_element_type=f32)
    lane = iota((8, 320), 1) >> 5
    cell = iota((8, 320), 0)
    weighted = tiled * lw
    for k in range(3):
        out = jnp.zeros((8, 320), f32)
        for q in range(3):
            n = (2 - k) * 3 + 2 - q
            taps = jnp.sum(weighted[n * 32 : n * 32 + 32], axis=0, keepdims=True)
            out = out + jnp.where(lane == cell + q, taps, 0.0)
        last[8 * k : 8 * k + 8, :] = out


def kernel(
    sizes, *refs,
):
    given, refs = refs[:10], refs[10:]
    (
        result,
        coeffs, basis, observed_own, lift_w, lift_b, w_one, b_one, w_two, b_two, read_w,
        pressure, grad, in_sem, out_sem,
        first, ahead, back, last, bias_two, read,
        gath, turned, basis_half, field, obs, stack, hid, gtwo, gone, press_ext, own, own_half,
        away, away_in, q_in, z_send, z_in,
        g_ss, g_rs, h_ss, h_rs, r_ss, r_rs,
    ) = refs
    R, N, Z, X, Y = sizes
    row, col = lax.axis_index("row"), lax.axis_index("col")
    z, x = row // X, row % X
    y, c = col // 2, col % 2
    mp = coeffs.shape[0]
    cells, modes = basis.shape

    local = (coeffs, basis, observed_own, lift_w, lift_b, w_one, b_one, w_two, b_two, read_w)
    fetch = [
        pltpu.make_async_copy(src, dst, in_sem.at[k]) for k, (src, dst) in enumerate(zip(given, local))
    ]
    for k in (0, 2, 3, 4, 5, 6, 7, 8, 9, 1):
        fetch[k].start()

    z_to = [((lax.rem(z + k, Z) * X + x, col), lax.rem(z + k, Z)) for k in range(1, Z)]
    Q = X * Y
    q = x * Y + y
    q_to = []
    for k in range(1, Q):
        p = lax.rem(q + k, Q)
        q_to.append(((z * X + p // Y, p % Y * 2 + c), p))
    c_to = (row, y * 2 + 1 - c)
    sides = [(dx, dy) for dx in (-1, 0, 1) for dy in (-1, 0, 1) if (dx, dy) != (0, 0)]

    def exists(dx, dy):
        return (row + dx >= 0) & (row + dx < R) & (col + dy >= 0) & (col + dy < N)

    field[...] = jnp.zeros(field.shape, f32)
    obs[...] = jnp.zeros(obs.shape, f32)

    barrier = pltpu.get_barrier_semaphore()
    expect = (Z - 1) + (Q - 1) + 1
    for dev in [d for d, _ in z_to + q_to] + [c_to]:
        pl.semaphore_signal(barrier, inc=1, device_id=dev, device_id_type=MESH)
    for dx, dy in sides:
        there = exists(dx, dy)

        @pl.when(there)
        def _():
            pl.semaphore_signal(
                barrier, inc=1, device_id=(row + dx, col + dy), device_id_type=MESH
            )

        expect = expect + there.astype(jnp.int32)
    fetch[0].wait()
    gath[z, q, c] = coeffs[...].astype(bf16)
    pl.semaphore_wait(barrier, expect)

    def push(src, dst, ss, rs, dev):
        copy = pltpu.make_async_remote_copy(
            src_ref=src, dst_ref=dst, send_sem=ss, recv_sem=rs, device_id=dev,
            device_id_type=MESH,
        )
        copy.start()
        return copy

    sent = []
    n_gath = [0]

    def spread(ref, peers):
        made = []
        for dev, _ in peers:
            k = n_gath[0]
            n_gath[0] += 1
            made.append(push(ref, ref, g_ss.at[k], g_rs.at[k], dev))
        sent.extend(made)
        return made

    def rim(buf, width, base):
        def parts(dx, dy):
            src = buf.at[1, pl.ds(width, 8)] if dx == 0 else (
                buf.at[1, pl.ds(width, width)] if dx < 0 else buf.at[1, pl.ds(8, width)]
            )
            at = pl.ds(width, 8) if dx == 0 else (
                pl.ds(8 + width, width) if dx < 0 else pl.ds(0, width)
            )
            return src, buf.at[1 - dy, at]

        def do(k, dx, dy):
            src, dst = parts(dx, dy)
            return pltpu.make_async_remote_copy(
                src_ref=src, dst_ref=dst, send_sem=h_ss.at[base + k],
                recv_sem=h_rs.at[base + k], device_id=(row + dx, col + dy),
                device_id_type=MESH,
            )

        def start():
            for k, (dx, dy) in enumerate(sides):
                @pl.when(exists(dx, dy))
                def _():
                    do(k, dx, dy).start()

        def wait_in():
            for k, (dx, dy) in enumerate(sides):
                @pl.when(exists(-dx, -dy))
                def _():
                    do(k, dx, dy).wait_recv()

        def wait_out():
            for k, (dx, dy) in enumerate(sides):
                @pl.when(exists(dx, dy))
                def _():
                    do(k, dx, dy).wait_send()

        return start, wait_in, wait_out

    came = [lax.rem(z - k + Z, Z) for k in range(Z)]
    stage = spread(gath.at[z, q, c], z_to)
    moving = [spread(gath.at[z, q, c], q_to)]
    fetch[2].wait()
    obs[1, 2:10] = observed_own[...]
    obs_start, obs_in, obs_out = rim(obs, 2, 0)
    obs_start()
    for k in range(3, 10):
        fetch[k].wait()
    build_first(lift_w, lift_b, w_one, b_one, b_two, read_w, first, bias_two, read)
    for k in range(1, Z):
        stage[k - 1].wait_recv()
        moving.append(spread(gath.at[came[k], q, c], q_to))
    build_others(lift_w, w_one, w_two, ahead, back, last)
    fetch[1].wait()

    def arrange(i):
        at = pl.multiple_of(i * 512, 512)
        part = basis[:, pl.ds(at, 512)]
        basis_half[:, pl.ds(at, 512)] = part.astype(bf16)
        turned[pl.ds(at, 512), :] = part.T.astype(bf16)

    done = []
    for k, made in enumerate(moving):
        for copy in made:
            copy.wait_recv()
        done.extend(spread(gath.at[came[k], :, c], [(c_to, None)]))
        if k == 0:
            pl.loop(0, modes // 512)(arrange)

    group = X * Y * 2 * mp
    own_field = jnp.zeros((cells, 128), f32)
    for k, copy in enumerate(done):
        copy.wait_recv()
        own_field = own_field + jnp.dot(
            basis_half[:, pl.ds(pl.multiple_of(came[k] * group, 128), group)],
            gath[came[k]].reshape(group, 128), preferred_element_type=f32,
        )
    field[1, 4:12] = own_field.reshape(8, 8, 128)
    field_start, field_in, field_out = rim(field, 4, 8)
    field_start()
    field_in()
    obs_in()
    field_out()
    obs_out()

    ones = jnp.ones((8, 128), f32)
    y_at = lax.broadcasted_iota(jnp.int32, (24, 128), 0) + (col * 8 - 8)
    y_in = (y_at >= 0) & (y_at < N * 8)

    @pl.loop(0, 16, unroll=2)
    def _(i):
        values = jnp.concatenate([field[0, i], field[1, i], field[2, i]], axis=0)
        hi = values.astype(bf16).astype(f32)
        xg = row * 8 + i - 4
        inside = jnp.where(y_in & (xg >= 0) & (xg < R * 8), 1.0, 0.0)
        full = jnp.concatenate([hi, values - hi, inside, ones], axis=0)
        stack[pl.ds(pl.multiple_of(i * 80, 16), 80), :] = full.astype(bf16)

    def inside(count, off, xg):
        at = lax.broadcasted_iota(jnp.int32, (count * 32, 128), 0)
        low = (off - col * 8) * 32
        high = jnp.where((xg >= 0) & (xg < R * 8), low + N * 256, -1)
        return (at >= low) & (at < high)

    @pl.loop(0, 14, unroll=2)
    def _(i):
        rows = stack[pl.ds(pl.multiple_of(i * 80, 16), 240), :]
        acc = jnp.dot(first[...], rows, preferred_element_type=f32)
        value = jnp.where(inside(14, 3, row * 8 + i - 3), jnp.tanh(acc), 0.0)
        hid[:, pl.ds(pl.multiple_of(i * 128, 128), 128)] = value.astype(bf16)

    def conv(w, src, starts, at):
        out = []
        for s in starts:
            acc = None
            for k in range(3):
                v = src[s * 32 : s * 32 + 192, pl.ds(pl.multiple_of(at + k * 128, 128), 256)]
                d = jnp.dot(w[k], v, preferred_element_type=f32)
                acc = d if acc is None else acc + d
            out.append(acc)
        return out

    @pl.loop(0, 6)
    def _(i):
        at = i * 256
        acc = jnp.concatenate(conv(ahead, hid, (0, 4, 8), at), axis=0)
        for s in range(2):
            xi = i * 2 + s
            t = jnp.tanh(acc[:, s * 128 : s * 128 + 128] + bias_two[...])
            pr = jnp.sum((t * read[...]).reshape(12, 32, 128), axis=1)
            seen = jnp.concatenate([obs[0, xi], obs[1, xi], obs[2, xi]], axis=0)[6:18]
            miss = jnp.broadcast_to((pr - seen)[:, None, :], (12, 32, 128)).reshape(384, 128)
            g = miss * read[...] * (1.0 - t * t)
            g = jnp.where(inside(12, 2, row * 8 + xi - 2), g, 0.0)
            gtwo[:, pl.ds(pl.multiple_of(at + s * 128, 128), 128)] = g.astype(bf16)
            press_ext[xi] = pr[2:10]

    pressure[...] = press_ext[2:10].reshape(64, 128)
    pressure_copy = pltpu.make_async_copy(pressure, result.at[pl.ds(0, 64)], out_sem.at[0])
    pressure_copy.start()

    @pl.loop(0, 5)
    def _(i):
        at = i * 256
        a0, a1, a2 = conv(back, gtwo, (0, 4, 6), at)
        acc = jnp.concatenate([a0, a1, a2[64:]], axis=0)
        for s in range(2):
            xi = i * 2 + s
            h = hid[64:384, pl.ds(pl.multiple_of(at + (2 + s) * 128, 128), 128)].astype(f32)
            g = acc[:, s * 128 : s * 128 + 128] * (1.0 - h * h)
            g = jnp.where(inside(10, 1, row * 8 + xi - 1), g, 0.0)
            gone[:, pl.ds(pl.multiple_of(at + s * 128, 128), 128)] = g.astype(bf16)

    parts = jnp.dot(last[...].astype(bf16), gone[...], preferred_element_type=f32)
    slabs = [
        sum(parts[8 * k : 8 * k + 8, (xi + k) * 128 : (xi + k + 1) * 128] for k in range(3))
        for xi in range(8)
    ]
    grad_field = jnp.concatenate(slabs, axis=0).astype(bf16)

    def project(core, at, into, kind):
        @pl.loop(0, X * Y, unroll=4)
        def _(j):
            rows = pl.multiple_of(((at * X * Y + j) * 2 + core) * mp, mp)
            d = jnp.dot(turned[pl.ds(rows, mp), :], grad_field, preferred_element_type=f32)
            into[at, j] = d.astype(kind)

    n_red = [0]

    def shed(pairs):
        made = []
        for src, dst, dev in pairs:
            i = n_red[0]
            n_red[0] += 1
            made.append(push(src, dst, r_ss.at[i], r_rs.at[i], dev))
        sent.extend(made)
        return made

    order = [lax.rem(z + k + 1, Z) for k in range(Z)]
    moving = []
    for at in order:
        project(1 - c, at, away, bf16)
        moving.append(shed([(away.at[at], away_in.at[at], c_to)]))
    for at in order:
        project(c, at, own, f32)
    both = []
    for at, made in zip(order, moving):
        made[0].wait_recv()
        total = own[at] + away_in[at].astype(f32)
        own[at] = total
        own_half[at] = total.astype(bf16)
        both.append(
            shed([(own_half.at[at, p], q_in.at[k, at], d) for k, (d, p) in enumerate(q_to)])
        )
    stage = []
    for n, (at, made) in enumerate(zip(order, both)):
        for copy in made:
            copy.wait_recv()
        part = own[at, q]
        for k in range(Q - 1):
            part = part + q_in[k, at].astype(f32)
        if n < Z - 1:
            z_send[at] = part.astype(bf16)
            stage.extend(shed([(z_send.at[at], z_in.at[n], z_to[n][0])]))
    total = part + prior_weight * coeffs[...]
    for k, copy in enumerate(stage):
        copy.wait_recv()
        total = total + z_in[k].astype(f32)
    grad[...] = total
    grad_copy = pltpu.make_async_copy(grad, result.at[pl.ds(64, mp)], out_sem.at[1])
    grad_copy.start()
    for copy in sent:
        copy.wait_send()
    pressure_copy.wait()
    grad_copy.wait()


def shards(sizes, coeffs, basis, observed, lift_w, lift_b, w_one, b_one, w_two, b_two, read_w):
    R, N, Z, X, Y = sizes
    mode_count, batch = basis.shape[2], coeffs.shape[1]
    own = coeffs.shape[0]
    mp = max(own, 16)
    flat = basis.reshape(64, mode_count)
    if mp != own:
        flat = jnp.pad(flat.reshape(64, R * N, own), ((0, 0), (0, 0), (0, mp - own)))
        flat = flat.reshape(64, R * N * mp)
        coeffs = jnp.pad(coeffs, ((0, mp - own), (0, 0)))
    modes = R * N * mp
    hbm = pl.BlockSpec(memory_space=pl.ANY)
    block = (mp, batch)
    Q = X * Y
    copies = (Z - 1) + Z * Q
    V = pltpu.VMEM
    result = pl.pallas_call(
        functools.partial(kernel, sizes),
        out_shape=jax.ShapeDtypeStruct((64 + mp, batch), f32),
        in_specs=[hbm] * 10,
        out_specs=hbm,
        scratch_shapes=[
            V((mp, batch), f32),
            V((64, modes), f32),
            V((8, 8, batch), f32),
            V((32,), f32),
            V((32,), f32),
            V((288, 32), bf16),
            V((32,), f32),
            V((288, 32), bf16),
            V((32,), f32),
            V((32,), f32),
            V((64, batch), f32),
            V((mp, batch), f32),
            pltpu.SemaphoreType.DMA((10,)),
            pltpu.SemaphoreType.DMA((2,)),
            V((448, 240), bf16),
            V((3, 128, 192), bf16),
            V((3, 128, 192), bf16),
            V((24, 320), f32),
            V((384, 128), f32),
            V((384, 128), f32),
            V((Z, Q, 2) + block, bf16),
            V((modes, 64), bf16),
            V((64, modes), bf16),
            V((3, 16, 8, batch), f32),
            V((3, 12, 8, batch), f32),
            V((16 * 80, batch), bf16),
            V((448, 14 * batch), bf16),
            V((384, 12 * batch), bf16),
            V((320, 10 * batch), bf16),
            V((12, 8, batch), f32),
            V((Z, Q) + block, f32),
            V((Z, Q) + block, bf16),
            V((Z, Q) + block, bf16),
            V((Z, Q) + block, bf16),
            V((Q - 1, Z) + block, bf16),
            V((Z,) + block, bf16),
            V((Z - 1,) + block, bf16),
            pltpu.SemaphoreType.DMA((copies,)),
            pltpu.SemaphoreType.DMA((copies,)),
            pltpu.SemaphoreType.DMA((16,)),
            pltpu.SemaphoreType.DMA((16,)),
            pltpu.SemaphoreType.DMA((copies,)),
            pltpu.SemaphoreType.DMA((copies,)),
        ],
        compiler_params=pltpu.CompilerParams(
            collective_id=0, has_side_effects=True, vmem_limit_bytes=56 * 1024 * 1024
        ),
    )(
        coeffs, flat, observed, lift_w, lift_b, w_one.reshape(288, 32), b_one,
        w_two.reshape(288, 32), b_two, read_w,
    )
    return result[:64].reshape(8, 8, batch), result[64 : 64 + own]


def solution(mesh):
    R, N = mesh.shape["row"], mesh.shape["col"]
    X = 1 << ((R.bit_length() - 1) // 2)
    sizes = (R, N, R // X, X, N // 2)
    return jax.shard_map(
        functools.partial(shards, sizes),
        mesh=mesh,
        in_specs=(
            P(("row", "col"), None),
            P("row", "col", None),
            P("row", "col", None),
            P(),
            P(),
            P(),
            P(),
            P(),
            P(),
            P(),
        ),
        out_specs=(P("row", "col", None), P(("row", "col"), None)),
        check_vma=False,
    )
```

```python
import functools

import jax
import jax.numpy as jnp
from jax import lax
from jax.experimental import pallas as pl
from jax.experimental.pallas import tpu as pltpu
from jax.sharding import PartitionSpec as P

prior_weight = 0.1
MESH = pl.DeviceIdType.MESH
bf16 = jnp.bfloat16
f32 = jnp.float32


def column(vec):
    shape = (32, 32)
    same = lax.broadcasted_iota(jnp.int32, shape, 0) == lax.broadcasted_iota(jnp.int32, shape, 1)
    row = jnp.broadcast_to(vec[...].reshape(1, 32), shape)
    return jnp.sum(jnp.where(same, row, 0.0), axis=1, keepdims=True)


def iota(shape, axis):
    return lax.broadcasted_iota(jnp.int32, shape, axis)


def build_first(lift_w, lift_b, w_one, b_one, b_two, read_w, first, bias_two, read):

    def wide(col):
        return jnp.broadcast_to(col[None], (12, 32, 128)).reshape(384, 128)

    bias_two[...] = wide(column(b_two))
    read[...] = wide(column(read_w))
    lw, lb, bias = column(lift_w), column(lift_b), column(b_one)
    lw, lb = jnp.concatenate([lw] * 9, axis=0), jnp.concatenate([lb] * 9, axis=0)
    one = w_one[...].astype(f32)
    r, lane = iota((288, 240), 0), iota((288, 240), 1)
    p = (r >= 96).astype(jnp.int32) + (r >= 192).astype(jnp.int32)
    at = lane - (80 * p + ((r - 96 * p) >> 5) + 4)
    hi = bias.astype(bf16).astype(f32)
    lane = iota((32, 240), 1)
    bias = jnp.where(lane == 72, hi, jnp.where(lane == 73, bias - hi, 0.0))
    for y in range(14):
        spread = jnp.where(
            (at == y) | (at == y + 24), lw, jnp.where(at == y + 48, lb, 0.0)
        )
        block = lax.dot_general(
            one, spread, (((0,), (0,)), ((), ())), precision=lax.Precision.HIGHEST,
            preferred_element_type=f32,
        )
        first[y * 32 : y * 32 + 32, :] = (block + bias).astype(bf16)


def build_others(lift_w, w_one, w_two, ahead, back, last):
    lw = jnp.concatenate([column(lift_w)] * 9, axis=0)
    for k in range(3):
        rows = w_two[k * 96 : k * 96 + 96, :]
        for y in range(4):
            move = jnp.where(iota((96, 192), 1) == iota((96, 192), 0) + 32 * y, 1.0, 0.0)
            ahead[k, y * 32 : y * 32 + 32, :] = lax.dot_general(
                rows, move.astype(bf16), (((0,), (0,)), ((), ())), preferred_element_type=f32
            ).astype(bf16)
        rows = w_two[(2 - k) * 96 : (2 - k) * 96 + 96, :]
        moved = []
        for n in range(6):
            move = jnp.where(iota((32, 192), 1) == iota((32, 192), 0) + 32 * n, 1.0, 0.0)
            moved.append(jnp.dot(rows, move.astype(bf16), preferred_element_type=f32))
        for y in range(4):
            back[k, y * 32 : y * 32 + 32, :] = sum(
                moved[y + q][(2 - q) * 32 : (2 - q) * 32 + 32] for q in range(3)
            ).astype(bf16)

    tile = jnp.where((iota((32, 320), 1) & 31) == iota((32, 320), 0), 1.0, 0.0).astype(bf16)
    tiled = jnp.dot(w_one[...], tile, preferred_element_type=f32)
    lane = iota((8, 320), 1) >> 5
    cell = iota((8, 320), 0)
    weighted = tiled * lw
    for k in range(3):
        out = jnp.zeros((8, 320), f32)
        for q in range(3):
            n = (2 - k) * 3 + 2 - q
            taps = jnp.sum(weighted[n * 32 : n * 32 + 32], axis=0, keepdims=True)
            out = out + jnp.where(lane == cell + q, taps, 0.0)
        last[8 * k : 8 * k + 8, :] = out


def kernel(
    sizes, *refs,
):
    given, refs = refs[:10], refs[10:]
    (
        pressure_out, grad_out,
        coeffs, basis, observed_own, lift_w, lift_b, w_one, b_one, w_two, b_two, read_w,
        pressure, grad, in_sem, out_sem,
        first, ahead, back, last, bias_two, read,
        gath, turned, basis_half, field, obs, stack, hid, gtwo, gone, press_ext, own, own_half,
        away, away_in, q_in, z_send, z_in,
        g_ss, g_rs, h_ss, h_rs, r_ss, r_rs,
    ) = refs
    R, N, Z, X, Y = sizes
    row, col = lax.axis_index("row"), lax.axis_index("col")
    z, x = row // X, row % X
    y, c = col // 2, col % 2
    mp = coeffs.shape[0]
    cells, modes = basis.shape

    local = (coeffs, basis, observed_own, lift_w, lift_b, w_one, b_one, w_two, b_two, read_w)
    fetch = [
        pltpu.make_async_copy(src, dst, in_sem.at[k]) for k, (src, dst) in enumerate(zip(given, local))
    ]
    for k in (0, 2, 3, 4, 5, 6, 7, 8, 9, 1):
        fetch[k].start()

    z_to = [((lax.rem(z + k, Z) * X + x, col), lax.rem(z + k, Z)) for k in range(1, Z)]
    Q = X * Y
    q = x * Y + y
    q_to = []
    for k in range(1, Q):
        p = lax.rem(q + k, Q)
        q_to.append(((z * X + p // Y, p % Y * 2 + c), p))
    c_to = (row, y * 2 + 1 - c)
    sides = [(dx, dy) for dx in (-1, 0, 1) for dy in (-1, 0, 1) if (dx, dy) != (0, 0)]

    def exists(dx, dy):
        return (row + dx >= 0) & (row + dx < R) & (col + dy >= 0) & (col + dy < N)

    field[...] = jnp.zeros(field.shape, f32)
    obs[...] = jnp.zeros(obs.shape, f32)

    barrier = pltpu.get_barrier_semaphore()
    expect = (Z - 1) + (Q - 1) + 1
    for dev in [d for d, _ in z_to + q_to] + [c_to]:
        pl.semaphore_signal(barrier, inc=1, device_id=dev, device_id_type=MESH)
    for dx, dy in sides:
        there = exists(dx, dy)

        @pl.when(there)
        def _():
            pl.semaphore_signal(
                barrier, inc=1, device_id=(row + dx, col + dy), device_id_type=MESH
            )

        expect = expect + there.astype(jnp.int32)
    fetch[0].wait()
    gath[z, q, c] = coeffs[...].astype(bf16)
    pl.semaphore_wait(barrier, expect)

    def push(src, dst, ss, rs, dev):
        copy = pltpu.make_async_remote_copy(
            src_ref=src, dst_ref=dst, send_sem=ss, recv_sem=rs, device_id=dev,
            device_id_type=MESH,
        )
        copy.start()
        return copy

    sent = []
    n_gath = [0]

    def spread(ref, peers):
        made = []
        for dev, _ in peers:
            k = n_gath[0]
            n_gath[0] += 1
            made.append(push(ref, ref, g_ss.at[k], g_rs.at[k], dev))
        sent.extend(made)
        return made

    def rim(buf, width, base):
        def parts(dx, dy):
            src = buf.at[1, pl.ds(width, 8)] if dx == 0 else (
                buf.at[1, pl.ds(width, width)] if dx < 0 else buf.at[1, pl.ds(8, width)]
            )
            at = pl.ds(width, 8) if dx == 0 else (
                pl.ds(8 + width, width) if dx < 0 else pl.ds(0, width)
            )
            return src, buf.at[1 - dy, at]

        def do(k, dx, dy):
            src, dst = parts(dx, dy)
            return pltpu.make_async_remote_copy(
                src_ref=src, dst_ref=dst, send_sem=h_ss.at[base + k],
                recv_sem=h_rs.at[base + k], device_id=(row + dx, col + dy),
                device_id_type=MESH,
            )

        def start():
            for k, (dx, dy) in enumerate(sides):
                @pl.when(exists(dx, dy))
                def _():
                    do(k, dx, dy).start()

        def wait_in():
            for k, (dx, dy) in enumerate(sides):
                @pl.when(exists(-dx, -dy))
                def _():
                    do(k, dx, dy).wait_recv()

        def wait_out():
            for k, (dx, dy) in enumerate(sides):
                @pl.when(exists(dx, dy))
                def _():
                    do(k, dx, dy).wait_send()

        return start, wait_in, wait_out

    came = [lax.rem(z - k + Z, Z) for k in range(Z)]
    stage = spread(gath.at[z, q, c], z_to)
    moving = [spread(gath.at[z, q, c], q_to)]
    fetch[2].wait()
    obs[1, 2:10] = observed_own[...]
    obs_start, obs_in, obs_out = rim(obs, 2, 0)
    obs_start()
    for k in range(3, 10):
        fetch[k].wait()
    build_first(lift_w, lift_b, w_one, b_one, b_two, read_w, first, bias_two, read)
    for k in range(1, Z):
        stage[k - 1].wait_recv()
        moving.append(spread(gath.at[came[k], q, c], q_to))
    build_others(lift_w, w_one, w_two, ahead, back, last)
    fetch[1].wait()

    def arrange(i):
        at = pl.multiple_of(i * 512, 512)
        part = basis[:, pl.ds(at, 512)]
        basis_half[:, pl.ds(at, 512)] = part.astype(bf16)
        turned[pl.ds(at, 512), :] = part.T.astype(bf16)

    done = []
    for k, made in enumerate(moving):
        for copy in made:
            copy.wait_recv()
        done.extend(spread(gath.at[came[k], :, c], [(c_to, None)]))
        if k == 0:
            pl.loop(0, modes // 512)(arrange)

    group = X * Y * 2 * mp
    own_field = jnp.zeros((cells, 128), f32)
    for k, copy in enumerate(done):
        copy.wait_recv()
        own_field = own_field + jnp.dot(
            basis_half[:, pl.ds(pl.multiple_of(came[k] * group, 128), group)],
            gath[came[k]].reshape(group, 128), preferred_element_type=f32,
        )
    field[1, 4:12] = own_field.reshape(8, 8, 128)
    field_start, field_in, field_out = rim(field, 4, 8)
    field_start()
    field_in()
    obs_in()
    field_out()
    obs_out()

    ones = jnp.ones((8, 128), f32)
    y_at = lax.broadcasted_iota(jnp.int32, (24, 128), 0) + (col * 8 - 8)
    y_in = (y_at >= 0) & (y_at < N * 8)

    @pl.loop(0, 16, unroll=8)
    def _(i):
        values = jnp.concatenate([field[0, i], field[1, i], field[2, i]], axis=0)
        hi = values.astype(bf16).astype(f32)
        xg = row * 8 + i - 4
        inside = jnp.where(y_in & (xg >= 0) & (xg < R * 8), 1.0, 0.0)
        full = jnp.concatenate([hi, values - hi, inside, ones], axis=0)
        stack[pl.ds(pl.multiple_of(i * 80, 16), 80), :] = full.astype(bf16)

    def inside(count, off, xg):
        at = lax.broadcasted_iota(jnp.int32, (count * 32, 128), 0)
        low = (off - col * 8) * 32
        high = jnp.where((xg >= 0) & (xg < R * 8), low + N * 256, -1)
        return (at >= low) & (at < high)

    @pl.loop(0, 14, unroll=7)
    def _(i):
        rows = stack[pl.ds(pl.multiple_of(i * 80, 16), 240), :]
        acc = jnp.dot(first[...], rows, preferred_element_type=f32)
        value = jnp.where(inside(14, 3, row * 8 + i - 3), jnp.tanh(acc), 0.0)
        hid[:, pl.ds(pl.multiple_of(i * 128, 128), 128)] = value.astype(bf16)

    def conv(w, src, starts, at):
        out = []
        for s in starts:
            acc = None
            for k in range(3):
                v = src[s * 32 : s * 32 + 192, pl.ds(pl.multiple_of(at + k * 128, 128), 256)]
                d = jnp.dot(w[k], v, preferred_element_type=f32)
                acc = d if acc is None else acc + d
            out.append(acc)
        return out

    @pl.loop(0, 6, unroll=6)
    def _(i):
        at = i * 256
        acc = jnp.concatenate(conv(ahead, hid, (0, 4, 8), at), axis=0)
        for s in range(2):
            xi = i * 2 + s
            t = jnp.tanh(acc[:, s * 128 : s * 128 + 128] + bias_two[...])
            pr = jnp.sum((t * read[...]).reshape(12, 32, 128), axis=1)
            seen = jnp.concatenate([obs[0, xi], obs[1, xi], obs[2, xi]], axis=0)[6:18]
            miss = jnp.broadcast_to((pr - seen)[:, None, :], (12, 32, 128)).reshape(384, 128)
            g = miss * read[...] * (1.0 - t * t)
            g = jnp.where(inside(12, 2, row * 8 + xi - 2), g, 0.0)
            gtwo[:, pl.ds(pl.multiple_of(at + s * 128, 128), 128)] = g.astype(bf16)
            press_ext[xi] = pr[2:10]

    pressure[...] = press_ext[2:10].reshape(64, 128)
    pressure_copy = pltpu.make_async_copy(pressure, pressure_out, out_sem.at[0])
    pressure_copy.start()

    @pl.loop(0, 5, unroll=5)
    def _(i):
        at = i * 256
        a0, a1, a2 = conv(back, gtwo, (0, 4, 6), at)
        acc = jnp.concatenate([a0, a1, a2[64:]], axis=0)
        for s in range(2):
            xi = i * 2 + s
            h = hid[64:384, pl.ds(pl.multiple_of(at + (2 + s) * 128, 128), 128)].astype(f32)
            g = acc[:, s * 128 : s * 128 + 128] * (1.0 - h * h)
            g = jnp.where(inside(10, 1, row * 8 + xi - 1), g, 0.0)
            gone[:, pl.ds(pl.multiple_of(at + s * 128, 128), 128)] = g.astype(bf16)

    parts = jnp.dot(last[...].astype(bf16), gone[...], preferred_element_type=f32)
    slabs = [
        sum(parts[8 * k : 8 * k + 8, (xi + k) * 128 : (xi + k + 1) * 128] for k in range(3))
        for xi in range(8)
    ]
    grad_field = jnp.concatenate(slabs, axis=0).astype(bf16)

    def project(core, at, into, kind):
        @pl.loop(0, X * Y, unroll=4)
        def _(j):
            rows = pl.multiple_of(((at * X * Y + j) * 2 + core) * mp, mp)
            d = jnp.dot(turned[pl.ds(rows, mp), :], grad_field, preferred_element_type=f32)
            into[at, j] = d.astype(kind)

    n_red = [0]

    def shed(pairs):
        made = []
        for src, dst, dev in pairs:
            i = n_red[0]
            n_red[0] += 1
            made.append(push(src, dst, r_ss.at[i], r_rs.at[i], dev))
        sent.extend(made)
        return made

    order = [lax.rem(z + k + 1, Z) for k in range(Z)]
    moving = []
    for at in order:
        project(1 - c, at, away, bf16)
        moving.append(shed([(away.at[at], away_in.at[at], c_to)]))
    for at in order:
        project(c, at, own, f32)
    both = []
    for at, made in zip(order, moving):
        made[0].wait_recv()
        total = own[at] + away_in[at].astype(f32)
        own[at] = total
        own_half[at] = total.astype(bf16)
        both.append(
            shed([(own_half.at[at, p], q_in.at[k, at], d) for k, (d, p) in enumerate(q_to)])
        )
    stage = []
    for n, (at, made) in enumerate(zip(order, both)):
        for copy in made:
            copy.wait_recv()
        part = own[at, q]
        for k in range(Q - 1):
            part = part + q_in[k, at].astype(f32)
        if n < Z - 1:
            z_send[at] = part.astype(bf16)
            stage.extend(shed([(z_send.at[at], z_in.at[n], z_to[n][0])]))
    total = part + prior_weight * coeffs[...]
    for k, copy in enumerate(stage):
        copy.wait_recv()
        total = total + z_in[k].astype(f32)
    grad[...] = total
    grad_copy = pltpu.make_async_copy(grad, grad_out, out_sem.at[1])
    grad_copy.start()
    for copy in sent:
        copy.wait_send()
    pressure_copy.wait()
    grad_copy.wait()


def shards(sizes, coeffs, basis, observed, lift_w, lift_b, w_one, b_one, w_two, b_two, read_w):
    R, N, Z, X, Y = sizes
    mode_count, batch = basis.shape[2], coeffs.shape[1]
    own = coeffs.shape[0]
    mp = max(own, 16)
    flat = basis.reshape(64, mode_count)
    if mp != own:
        flat = jnp.pad(flat.reshape(64, R * N, own), ((0, 0), (0, 0), (0, mp - own)))
        flat = flat.reshape(64, R * N * mp)
        coeffs = jnp.pad(coeffs, ((0, mp - own), (0, 0)))
    modes = R * N * mp
    hbm = pl.BlockSpec(memory_space=pl.ANY)
    block = (mp, batch)
    Q = X * Y
    copies = (Z - 1) + Z * Q
    V = pltpu.VMEM
    pressure, grad = pl.pallas_call(
        functools.partial(kernel, sizes),
        out_shape=(
            jax.ShapeDtypeStruct((64, batch), f32),
            jax.ShapeDtypeStruct((mp, batch), f32),
        ),
        in_specs=[hbm] * 10,
        out_specs=(hbm, hbm),
        scratch_shapes=[
            V((mp, batch), f32),
            V((64, modes), f32),
            V((8, 8, batch), f32),
            V((32,), f32),
            V((32,), f32),
            V((288, 32), bf16),
            V((32,), f32),
            V((288, 32), bf16),
            V((32,), f32),
            V((32,), f32),
            V((64, batch), f32),
            V((mp, batch), f32),
            pltpu.SemaphoreType.DMA((10,)),
            pltpu.SemaphoreType.DMA((2,)),
            V((448, 240), bf16),
            V((3, 128, 192), bf16),
            V((3, 128, 192), bf16),
            V((24, 320), f32),
            V((384, 128), f32),
            V((384, 128), f32),
            V((Z, Q, 2) + block, bf16),
            V((modes, 64), bf16),
            V((64, modes), bf16),
            V((3, 16, 8, batch), f32),
            V((3, 12, 8, batch), f32),
            V((16 * 80, batch), bf16),
            V((448, 14 * batch), bf16),
            V((384, 12 * batch), bf16),
            V((320, 10 * batch), bf16),
            V((12, 8, batch), f32),
            V((Z, Q) + block, f32),
            V((Z, Q) + block, bf16),
            V((Z, Q) + block, bf16),
            V((Z, Q) + block, bf16),
            V((Q - 1, Z) + block, bf16),
            V((Z,) + block, bf16),
            V((Z - 1,) + block, bf16),
            pltpu.SemaphoreType.DMA((copies,)),
            pltpu.SemaphoreType.DMA((copies,)),
            pltpu.SemaphoreType.DMA((16,)),
            pltpu.SemaphoreType.DMA((16,)),
            pltpu.SemaphoreType.DMA((copies,)),
            pltpu.SemaphoreType.DMA((copies,)),
        ],
        compiler_params=pltpu.CompilerParams(
            collective_id=0, has_side_effects=True, vmem_limit_bytes=56 * 1024 * 1024
        ),
    )(
        coeffs, flat, observed, lift_w, lift_b, w_one.reshape(288, 32), b_one,
        w_two.reshape(288, 32), b_two, read_w,
    )
    return pressure.reshape(8, 8, batch), grad[:own]


def solution(mesh):
    R, N = mesh.shape["row"], mesh.shape["col"]
    X = 1 << ((R.bit_length() - 1) // 2)
    sizes = (R, N, R // X, X, N // 2)
    return jax.shard_map(
        functools.partial(shards, sizes),
        mesh=mesh,
        in_specs=(
            P(("row", "col"), None),
            P("row", "col", None),
            P("row", "col", None),
            P(),
            P(),
            P(),
            P(),
            P(),
            P(),
            P(),
        ),
        out_specs=(P("row", "col", None), P(("row", "col"), None)),
        check_vma=False,
    )
```
